512 devices in a mesh: blk: 256 (over y, x, z), pair: 2 (over core).
Axes of the slice: x: 4, y: 4, z: 16, core: 2. Of those that a mesh axis runs over, the one named last changes fastest.
Arguments:
- features: bfloat16 [524288, 128], P('blk'), may hold values from -6 to 6
- subspace: float32 [128, 524288], P(None, 'blk'), may hold values from -18 to 18
- offsets: int32 [2, 256], P('pair', 'blk'), may hold values from -3 to 3, as said below
- counts: int32 [2, 256], P('pair', 'blk'), may hold values from 1 to 2048
Outputs:
- new_field: float32 [128, 524288], P(None, 'blk')
- ritz_gram: float32 [128, 128], replicated
The draws below stay inside these ranges and needn't reach their ends.
Inputs may be any that keep to these rules, and one draw needn't show every extreme that they name: offsets are never 0 and b + offsets[r, b] is always one of the 256 blocks.
All inputs are finite; a program needn't handle non-finite values.
Results may differ from the reference program's by a relative error of at most 0.003.
The reference program's roundings to bfloat16 on the way count: a program that leaves them out, or rounds other values in their place, can miss the bound.
Values may be sent and summed in bfloat16 or wider, within the bound.
No kernel may reach another device: no remote copies, remote signals or barrier semaphores. Data moves between devices by JAX's collectives and lax.ppermute only.
A program may use at most 64 MiB of HBM per device.

```python
import jax
import jax.numpy as jnp
from jax import lax

FEAT = 128
SUB = 128
PART_DEV = 2048
REACH = 3
BLOCKS = 256
ROUNDS = 2
PARTICLES = 524288


def draw_subspace(key, part):
    key = jax.random.fold_in(key, 3)
    ramp = 1.0 + 2.0 * jnp.arange(PARTICLES, dtype=jnp.float32) / float(PARTICLES - 1)
    base = jnp.clip(jax.random.normal(key, (SUB, PARTICLES), jnp.float32), -6.0, 6.0)
    return base * ramp[None, :]


def draw_offsets(key, part):
    key = jax.random.fold_in(key, 1)
    first_key = jax.random.fold_in(key, 11)
    second_key = jax.random.fold_in(key, 12)
    magnitude = jax.random.randint(first_key, (ROUNDS, BLOCKS), 1, REACH + 1, dtype=jnp.int32)
    signs = jax.random.randint(second_key, (ROUNDS, BLOCKS), 0, 2, dtype=jnp.int32) * 2 - 1
    moves = magnitude * signs
    position = jnp.arange(BLOCKS, dtype=jnp.int32)[None, :]
    target = position + moves
    moves = jnp.where((target < 0) | (target >= BLOCKS), -moves, moves)
    moves = moves.at[0, 0].set(REACH)
    moves = moves.at[ROUNDS - 1, BLOCKS - 1].set(-REACH)
    return moves.astype(jnp.int32)


def draw_counts(key, part):
    key = jax.random.fold_in(key, 2)
    drawn = jax.random.randint(key, (ROUNDS, BLOCKS), 1, PART_DEV + 1, dtype=jnp.int32)
    drawn = drawn.at[0, BLOCKS // 2].set(PART_DEV)
    return drawn.astype(jnp.int32)


def block_scale(stream_key, extent, shards, least, largest):
    gain = 1.0
    for axis_at, parts in shards:
        steps = jax.random.uniform(jax.random.fold_in(jax.random.fold_in(stream_key, 6), axis_at), (parts,), jnp.float32, least / len(shards), largest / len(shards))
        gain = gain * jnp.repeat(jnp.exp(steps), extent[axis_at] // parts).reshape((-1,) + (1,) * (len(extent) - 1 - axis_at))
    return gain


def centred(key, shape, width, reach, cuts=(), kind=jnp.bfloat16):
    values = jax.random.normal(key, shape, jnp.float32) * width
    if len(cuts) > 0:
        values = block_scale(key, shape, cuts, -0.22, 0.18) * values
    return jnp.clip(values, min=-reach, max=reach).astype(kind)


def setup_inputs(seed: int = 0) -> dict:
    key_of = jax.random.split(jax.random.key(seed), 5)
    features = centred(key_of[0], (PARTICLES, FEAT), 1.0, 6.0, ((0, 256),))
    subspace = draw_subspace(jax.random.fold_in(key_of[4], 71), 0)
    offsets = draw_offsets(jax.random.fold_in(key_of[4], 71), 0)
    counts = draw_counts(jax.random.fold_in(key_of[4], 71), 0)
    return dict(features=features, subspace=subspace, offsets=offsets, counts=counts)


def kernel_apply(particles, columns, col_values, col_keep, row_ids, col_ids):
    kernel_width = 2.0 * particles.shape[1]
    row_norms = jnp.sum(jnp.square(particles.astype(jnp.float32)), axis=1)
    col_norms = jnp.sum(jnp.square(columns.astype(jnp.float32)), axis=1)
    inner_prod = jnp.dot(particles, columns.T, preferred_element_type=jnp.float32)
    distance_sq = row_norms[:, None] + col_norms[None, :] - 2.0 * inner_prod
    distinct = (row_ids[:, None] != col_ids[None, :]).astype(jnp.float32)
    weight = jnp.exp(-distance_sq / kernel_width) * col_keep[None, :] * distinct
    degree = jnp.sum(weight, axis=1)
    weighted = lax.dot_general(col_values, weight.astype(jnp.bfloat16), (((1,), (1,)), ((), ())), preferred_element_type=jnp.float32)
    return weighted, degree


def reference(features, subspace, offsets, counts):
    values = subspace.astype(jnp.bfloat16)
    row_ids = jnp.arange(PART_DEV, dtype=jnp.int32)
    no_ids = jnp.full((PART_DEV,), -1, dtype=jnp.int32)
    all_keep = jnp.ones((PART_DEV,), jnp.float32)

    def per_block(block_index):
        start = (block_index * PART_DEV).astype(jnp.int32)
        own_feats = lax.dynamic_slice_in_dim(features, start, PART_DEV, 0)
        own_values = lax.dynamic_slice_in_dim(values, start, PART_DEV, 1)
        weighted, degree = kernel_apply(own_feats, own_feats, own_values, all_keep, row_ids, row_ids)
        for round_index in range(ROUNDS):
            partner = (block_index + offsets[round_index, block_index]).astype(jnp.int32)
            other_start = (partner * PART_DEV).astype(jnp.int32)
            other_feats = lax.dynamic_slice_in_dim(features, other_start, PART_DEV, 0)
            other_values = lax.dynamic_slice_in_dim(values, other_start, PART_DEV, 1)
            col_keep = (row_ids < counts[round_index, block_index]).astype(jnp.float32)
            extra_sum, extra_deg = kernel_apply(own_feats, other_feats, other_values, col_keep, row_ids, no_ids)
            weighted = weighted + extra_sum
            degree = degree + extra_deg
        return weighted / degree[None, :]

    blocks_out = lax.map(per_block, jnp.arange(BLOCKS, dtype=jnp.int32))
    new_field = jnp.transpose(blocks_out, (1, 0, 2)).reshape(SUB, PARTICLES)
    ritz_gram = jnp.dot(new_field, new_field.T, precision=lax.Precision.HIGHEST, preferred_element_type=jnp.float32) / float(PARTICLES)
    return new_field, ritz_gram
```

```python
import functools

import jax
import jax.numpy as jnp
from jax import lax
from jax.experimental import pallas as pl
from jax.experimental.pallas import tpu as pltpu
from jax.sharding import PartitionSpec as P

REACH = 3
CHUNKS = 2
TILE = 256
FAR = 1e30
NT = (((1,), (1,)), ((), ()))
PARAMS = pltpu.CompilerParams(vmem_limit_bytes=40 * 2**20)


def pack_kernel(core_ref, feats_ref, field_ref, *packed_refs):
    rows = feats_ref.shape[0] // CHUNKS
    for chunk, packed_ref in enumerate(packed_refs):
        packed_ref[:rows, :] = feats_ref[chunk * rows : (chunk + 1) * rows, :]
        for at in range(0, rows, 128):
            start = chunk * rows + at
            packed_ref[rows + at : rows + at + 128, :] = field_ref[:, start : start + 128].astype(
                jnp.bfloat16
            )


def pack(core, features, subspace):
    block, feat = features.shape
    sub = subspace.shape[0]
    half = block // 2
    piece = jax.ShapeDtypeStruct((block // CHUNKS, feat), jnp.bfloat16)
    return pl.pallas_call(
        pack_kernel,
        grid_spec=pltpu.PrefetchScalarGridSpec(
            num_scalar_prefetch=1,
            grid=(1,),
            in_specs=[
                pl.BlockSpec((half, feat), lambda i, core: (core[0], 0)),
                pl.BlockSpec((sub, half), lambda i, core: (0, core[0])),
            ],
            out_specs=[pl.BlockSpec(piece.shape, lambda i, core: (0, 0))] * CHUNKS,
        ),
        out_shape=[piece] * CHUNKS,
        compiler_params=PARAMS,
        cost_estimate=pl.CostEstimate(flops=0, bytes_accessed=2 * 2**20, transcendentals=0),
        name="pack",
    )(core, features, subspace)


def norms_of(part):
    wide = part.astype(jnp.float32)
    return jnp.sum(wide * wide, axis=1, keepdims=True) * (1.0 / 256.0)


def add_columns(feats, vals, col_norms, rows_t, row_norms, acc, deg, apart=None):
    inner = jnp.dot(feats, rows_t, preferred_element_type=jnp.float32)
    weight = jnp.exp(inner - col_norms - row_norms)
    if apart is not None:
        weight = jnp.where(apart, weight, 0.0)
    deg[...] += jnp.sum(weight.reshape(TILE // 8, 8, weight.shape[1]), axis=0)
    acc[...] += jnp.dot(vals, weight.astype(jnp.bfloat16), preferred_element_type=jnp.float32)


def side_by_side(read, start):
    return jnp.concatenate([read(start), read(start + 128)], axis=1)


def self_kernel(core_ref, feats_ref, *refs):
    packed = refs[:CHUNKS]
    acc, deg, rows_t, row_norms = refs[CHUNKS:]
    block = feats_ref.shape[0]
    for at in range(0, block, TILE):
        wide = feats_ref[at : at + TILE, :].astype(jnp.float32).T
        row_norms[:, at : at + TILE] = jnp.sum(wide * wide, axis=0, keepdims=True) * (1.0 / 256.0)
        rows_t[:, at : at + TILE] = (wide * (1.0 / 128.0)).astype(jnp.bfloat16)
    acc[...] = jnp.zeros_like(acc)
    deg[...] = jnp.zeros_like(deg)
    cols = packed[0].shape[0] // 2
    for chunk in range(CHUNKS):
        held = packed[chunk]

        @pl.loop(0, cols // TILE)
        def _(step):
            at = pl.multiple_of(step * TILE, TILE)
            feats = held[pl.ds(at, TILE), :]
            vals = side_by_side(
                lambda start: held[pl.ds(pl.multiple_of(start, 128), 128), :], cols + at
            )
            first = core_ref[0] * (block // 2) + chunk * cols + at
            col_ids = first + lax.broadcasted_iota(jnp.int32, (TILE, block), 0)
            row_ids = lax.broadcasted_iota(jnp.int32, (TILE, block), 1)
            add_columns(
                feats, vals, norms_of(feats), rows_t[...], row_norms[...], acc, deg, col_ids != row_ids
            )


def apply_self(core, features, packed):
    block, feat = features.shape
    outs = [
        jax.ShapeDtypeStruct((feat, block), jnp.float32),
        jax.ShapeDtypeStruct((8, block), jnp.float32),
        jax.ShapeDtypeStruct((feat, block), jnp.bfloat16),
        jax.ShapeDtypeStruct((1, block), jnp.float32),
    ]
    whole = lambda i, core: (0, 0)
    return pl.pallas_call(
        self_kernel,
        grid_spec=pltpu.PrefetchScalarGridSpec(
            num_scalar_prefetch=1,
            grid=(1,),
            in_specs=[pl.BlockSpec(x.shape, whole) for x in (features, *packed)],
            out_specs=[pl.BlockSpec(x.shape, whole) for x in outs],
        ),
        out_shape=outs,
        compiler_params=PARAMS,
        cost_estimate=pl.CostEstimate(
            flops=2 * 2 * block * block // 2 * feat,
            bytes_accessed=4 * 2**20,
            transcendentals=block * block // 2,
        ),
        name="own_block",
    )(core, features, *packed)


def partner_kernel(scalars, rows_t, row_norms, own_acc, own_deg, *refs):
    near = refs[: 2 * REACH * CHUNKS]
    acc, deg, held, sems = refs[2 * REACH * CHUNKS :]
    cols = held.shape[2] // 2
    for turn in range(2):
        for slot in range(2 * REACH):

            @pl.when(scalars[turn] == slot)
            def _():
                for chunk in range(CHUNKS):
                    pltpu.make_async_copy(
                        near[slot * CHUNKS + chunk], held.at[turn, chunk], sems.at[turn, chunk]
                    ).start()

    acc[...] = own_acc[...]
    deg[...] = own_deg[...]
    for turn in range(2):
        for chunk in range(CHUNKS):
            pltpu.make_async_copy(near[chunk], held.at[turn, chunk], sems.at[turn, chunk]).wait()
            first = scalars[4] * (CHUNKS * cols) + chunk * cols

            @pl.loop(0, cols // TILE)
            def _(step):
                at = pl.multiple_of(step * TILE, TILE)
                feats = held[turn, chunk, pl.ds(at, TILE), :]
                vals = side_by_side(
                    lambda start: held[turn, chunk, pl.ds(pl.multiple_of(start, 128), 128), :],
                    cols + at,
                )
                ids = first + at + lax.broadcasted_iota(jnp.int32, (TILE, 1), 0)
                norms = jnp.where(ids < scalars[2 + turn], norms_of(feats), FAR)
                add_columns(feats, vals, norms, rows_t[...], row_norms[...], acc, deg)


def apply_partners(scalars, rows_t, row_norms, own_acc, own_deg, near):
    feat, block = rows_t.shape
    half = block // 2
    outs = [
        jax.ShapeDtypeStruct((feat, half), jnp.float32),
        jax.ShapeDtypeStruct((8, half), jnp.float32),
    ]
    picked = lambda i, scalars: (0, scalars[5])
    whole = lambda i, scalars: (0, 0)
    return pl.pallas_call(
        partner_kernel,
        grid_spec=pltpu.PrefetchScalarGridSpec(
            num_scalar_prefetch=1,
            grid=(1,),
            in_specs=[
                pl.BlockSpec((feat, half), picked),
                pl.BlockSpec((1, half), picked),
                pl.BlockSpec((feat, half), picked),
                pl.BlockSpec((8, half), picked),
            ]
            + [pl.BlockSpec(memory_space=pl.ANY)] * len(near),
            out_specs=[pl.BlockSpec(x.shape, whole) for x in outs],
            scratch_shapes=[
                pltpu.VMEM((2, CHUNKS, *near[0].shape), jnp.bfloat16),
                pltpu.SemaphoreType.DMA((2, CHUNKS)),
            ],
        ),
        out_shape=outs,
        compiler_params=PARAMS,
        cost_estimate=pl.CostEstimate(
            flops=2 * 2 * half * block * feat,
            bytes_accessed=3 * 2**20,
            transcendentals=half * block,
        ),
        name="partners",
    )(scalars, rows_t, row_norms, own_acc, own_deg, *near)


def field_kernel(acc, deg, far_acc, far_deg, field, gram):
    degree = jnp.sum(deg[...] + far_deg[...], axis=0, keepdims=True)
    field[...] = (acc[...] + far_acc[...]) / degree
    gram[...] = lax.dot_general(
        field[...],
        field[...],
        NT,
        precision=lax.Precision.HIGHEST,
        preferred_element_type=jnp.float32,
    )


def make_field(acc, deg, far_acc, far_deg):
    sub = acc.shape[0]
    outs = [
        jax.ShapeDtypeStruct(acc.shape, jnp.float32),
        jax.ShapeDtypeStruct((sub, sub), jnp.float32),
    ]
    return pl.pallas_call(
        field_kernel,
        out_shape=outs,
        compiler_params=PARAMS,
        cost_estimate=pl.CostEstimate(
            flops=12 * sub * sub * acc.shape[1], bytes_accessed=2 * 2**20, transcendentals=0
        ),
        name="field",
    )(acc, deg, far_acc, far_deg)


def join_kernel(core_ref, own, other, out):
    @pl.when(pl.program_id(0) == core_ref[0])
    def _():
        out[...] = own[...]

    @pl.when(pl.program_id(0) != core_ref[0])
    def _():
        out[...] = other[...]


def join(core, own, other):
    sub, half = own.shape
    return pl.pallas_call(
        join_kernel,
        grid_spec=pltpu.PrefetchScalarGridSpec(
            num_scalar_prefetch=1,
            grid=(2,),
            in_specs=[pl.BlockSpec((sub, half), lambda i, core: (0, 0))] * 2,
            out_specs=pl.BlockSpec((sub, half), lambda i, core: (0, i)),
        ),
        out_shape=jax.ShapeDtypeStruct((sub, 2 * half), jnp.float32),
        compiler_params=PARAMS,
        cost_estimate=pl.CostEstimate(flops=0, bytes_accessed=2 * 2**20, transcendentals=0),
        name="join",
    )(core, own, other)


def swap(x):
    return lax.ppermute(x, "pair", [(0, 1), (1, 0)])


def shift(x, by):
    length = lax.axis_size("blk")
    return lax.ppermute(x, "blk", [(i, (i + by) % length) for i in range(length)])


def slot_of(distance):
    return distance + REACH - (distance > 0).astype(jnp.int32)


def per_device(features, subspace, offsets, counts):
    block = features.shape[0]
    core = lax.axis_index("pair").astype(jnp.int32)
    core_arg = core.reshape(1)
    here = jnp.concatenate([slot_of(offsets), counts], axis=1)
    there = swap(here)
    packed = pack(core_arg, features, subspace)
    up, down = [list(packed)], [list(packed)]
    for _ in range(REACH):
        up.append([shift(x, 1) for x in up[-1]])
        down.append([shift(x, -1) for x in down[-1]])
    near = up[3] + up[2] + up[1] + down[1] + down[2] + down[3]
    own_acc, own_deg, rows_t, row_norms = apply_self(core_arg, features, packed)
    table = jnp.stack([here[0, 0], there[0, 0], here[0, 1], there[0, 1], core])
    sums = {}
    for name, half in (("far", 1 - core), ("near", core)):
        scalars = jnp.concatenate([table, half.reshape(1)])
        sums[name] = apply_partners(scalars, rows_t, row_norms, own_acc, own_deg, near)
        if name == "far":
            far_acc, far_deg = [swap(x) for x in sums["far"]]
    field, gram = make_field(*sums["near"], far_acc, far_deg)
    other = swap(field)
    total = lax.psum(gram.reshape(-1), ("blk", "pair")).reshape(gram.shape)
    ritz_gram = total * (1.0 / float(lax.axis_size("blk") * block))
    return (join(core_arg, field, other), ritz_gram)


def solution(mesh):
    placed = (P("blk", None), P(None, "blk"), P("pair", "blk"), P("pair", "blk"))
    return jax.shard_map(
        per_device, mesh=mesh, in_specs=placed, out_specs=(P(None, "blk"), P()), check_vma=False
    )
```

```python
import functools

import jax
import jax.numpy as jnp
from jax import lax
from jax.experimental import pallas as pl
from jax.experimental.pallas import tpu as pltpu
from jax.sharding import PartitionSpec as P

REACH = 3
TILE = 256
FAR = 1e30
NT = (((1,), (1,)), ((), ()))
PARAMS = pltpu.CompilerParams(vmem_limit_bytes=32 * 2**20)


def pack_kernel(core_ref, feats_ref, field_ref, packed_ref, field_part, sems):
    half, feat = feats_ref.shape[0] // 2, feats_ref.shape[1]
    start = pl.multiple_of(core_ref[0] * half, half)
    feats_copy = pltpu.make_async_copy(
        feats_ref.at[pl.ds(start, half), :], packed_ref.at[pl.ds(0, half), :], sems.at[0]
    )
    field_copy = pltpu.make_async_copy(field_ref.at[:, pl.ds(start, half)], field_part, sems.at[1])
    feats_copy.start()
    field_copy.start()
    field_copy.wait()
    for at in range(0, half, feat):
        packed_ref[half + at : half + at + feat, :] = field_part[:, at : at + feat].astype(
            jnp.bfloat16
        )
    feats_copy.wait()


def pack(core, features, subspace):
    block, feat = features.shape
    sub = subspace.shape[0]
    return pl.pallas_call(
        pack_kernel,
        grid_spec=pltpu.PrefetchScalarGridSpec(
            num_scalar_prefetch=1,
            grid=(1,),
            in_specs=[pl.BlockSpec(memory_space=pltpu.HBM)] * 2,
            out_specs=pl.BlockSpec((block, feat), lambda i, core: (0, 0)),
            scratch_shapes=[
                pltpu.VMEM((sub, block // 2), jnp.float32),
                pltpu.SemaphoreType.DMA((2,)),
            ],
        ),
        out_shape=jax.ShapeDtypeStruct((block, feat), jnp.bfloat16),
        compiler_params=PARAMS,
        cost_estimate=pl.CostEstimate(flops=0, bytes_accessed=2 * 2**20, transcendentals=0),
        name="pack",
    )(core, features, subspace)


def norms_of(part):
    wide = part.astype(jnp.float32)
    return jnp.sum(wide * wide, axis=1, keepdims=True) * (1.0 / 256.0)


def add_columns(feats, vals, col_norms, rows_t, row_norms, sums, apart=None):
    sub = vals.shape[0]
    inner = jnp.dot(feats, rows_t, preferred_element_type=jnp.float32)
    weight = jnp.exp(inner - col_norms - row_norms)
    if apart is not None:
        weight = jnp.where(apart, weight, 0.0)
    sums[sub:, :] += jnp.sum(weight.reshape(TILE // 8, 8, weight.shape[1]), axis=0)
    sums[:sub, :] += jnp.dot(vals, weight.astype(jnp.bfloat16), preferred_element_type=jnp.float32)


def values_at(held, start):
    first = held[pl.ds(pl.multiple_of(start, 128), 128), :]
    second = held[pl.ds(pl.multiple_of(start + 128, 128), 128), :]
    return jnp.concatenate([first, second], axis=1)


def self_kernel(core_ref, feats_ref, packed, sums, rows_t, row_norms, feats, sem):
    block = feats_ref.shape[0]
    half = block // 2
    copy = pltpu.make_async_copy(feats_ref, feats, sem)
    copy.start()
    sums[...] = jnp.zeros_like(sums)
    copy.wait()
    for at in range(0, block, TILE):
        wide = feats[at : at + TILE, :].astype(jnp.float32).T
        row_norms[:, at : at + TILE] = jnp.sum(wide * wide, axis=0, keepdims=True) * (1.0 / 256.0)
        rows_t[:, at : at + TILE] = (wide * (1.0 / 128.0)).astype(jnp.bfloat16)

    @pl.loop(0, half // TILE)
    def _(step):
        at = pl.multiple_of(step * TILE, TILE)
        part = packed[pl.ds(at, TILE), :]
        col_ids = core_ref[0] * half + at + lax.broadcasted_iota(jnp.int32, (TILE, block), 0)
        row_ids = lax.broadcasted_iota(jnp.int32, (TILE, block), 1)
        add_columns(
            part,
            values_at(packed, half + at),
            norms_of(part),
            rows_t[...],
            row_norms[...],
            sums,
            col_ids != row_ids,
        )


def apply_self(core, features, packed):
    block, feat = features.shape
    outs = [
        jax.ShapeDtypeStruct((feat + 8, block), jnp.float32),
        jax.ShapeDtypeStruct((feat, block), jnp.bfloat16),
        jax.ShapeDtypeStruct((1, block), jnp.float32),
    ]
    whole = lambda i, core: (0, 0)
    return pl.pallas_call(
        self_kernel,
        grid_spec=pltpu.PrefetchScalarGridSpec(
            num_scalar_prefetch=1,
            grid=(1,),
            in_specs=[pl.BlockSpec(memory_space=pltpu.HBM), pl.BlockSpec(packed.shape, whole)],
            out_specs=[pl.BlockSpec(x.shape, whole) for x in outs],
            scratch_shapes=[pltpu.VMEM((block, feat), jnp.bfloat16), pltpu.SemaphoreType.DMA],
        ),
        out_shape=outs,
        compiler_params=PARAMS,
        cost_estimate=pl.CostEstimate(
            flops=2 * 2 * block * block // 2 * feat,
            bytes_accessed=4 * 2**20,
            transcendentals=block * block // 2,
        ),
        name="own_block",
    )(core, features, packed)


def partner_kernel(core_ref, here, there, rows_t, row_norms, own_sums, *refs):
    near = refs[: 2 * REACH]
    sums, held, sems = refs[2 * REACH :]
    half = held.shape[1] // 2
    picks = (here, there)
    for turn in range(2):
        for slot in range(2 * REACH):

            @pl.when(picks[turn][0, 0] == slot)
            def _():
                pltpu.make_async_copy(near[slot], held.at[turn], sems.at[turn]).start()

    sums[...] = own_sums[...]
    for turn in range(2):
        pltpu.make_async_copy(near[0], held.at[turn], sems.at[turn]).wait()

        @pl.loop(0, half // TILE)
        def _(step):
            at = pl.multiple_of(step * TILE, TILE)
            part = held[turn, pl.ds(at, TILE), :]
            ids = core_ref[0] * half + at + lax.broadcasted_iota(jnp.int32, (TILE, 1), 0)
            norms = jnp.where(ids < picks[turn][0, 1], norms_of(part), FAR)
            vals = values_at(held.at[turn], half + at)
            add_columns(part, vals, norms, rows_t[...], row_norms[...], sums)


def apply_partners(which, core, here, there, rows_t, row_norms, own_sums, near):
    feat, block = rows_t.shape
    half = block // 2
    if which == "far":
        picked = lambda i, core, here, there: (0, 1 - core[0])
    else:
        picked = lambda i, core, here, there: (0, core[0])
    out = jax.ShapeDtypeStruct((feat + 8, half), jnp.float32)
    return pl.pallas_call(
        partner_kernel,
        grid_spec=pltpu.PrefetchScalarGridSpec(
            num_scalar_prefetch=3,
            grid=(1,),
            in_specs=[
                pl.BlockSpec((feat, half), picked),
                pl.BlockSpec((1, half), picked),
                pl.BlockSpec((feat + 8, half), picked),
            ]
            + [pl.BlockSpec(memory_space=pl.ANY)] * len(near),
            out_specs=pl.BlockSpec(out.shape, lambda i, core, here, there: (0, 0)),
            scratch_shapes=[
                pltpu.VMEM((2, *near[0].shape), jnp.bfloat16),
                pltpu.SemaphoreType.DMA((2,)),
            ],
        ),
        out_shape=out,
        compiler_params=PARAMS,
        cost_estimate=pl.CostEstimate(
            flops=2 * 2 * half * block * feat,
            bytes_accessed=3 * 2**20,
            transcendentals=half * block,
        ),
        name="partners_" + which,
    )(core, here, there, rows_t, row_norms, own_sums, *near)


def field_kernel(scale, sums, far_sums, field, upper):
    sub = field.shape[0]
    mid, low = sub // 2, sub // 4
    degree = jnp.sum(sums[sub:, :] + far_sums[sub:, :], axis=0, keepdims=True)
    field[...] = (sums[:sub, :] + far_sums[:sub, :]) / degree
    gram = lax.dot_general(
        field[...],
        field[...],
        NT,
        precision=lax.Precision.HIGHEST,
        preferred_element_type=jnp.float32,
    )
    gram = gram * scale
    upper[:mid, :] = gram[:mid, :]
    upper[mid:, :] = jnp.concatenate([gram[mid : mid + low, mid:], gram[mid + low :, mid:]], axis=1)


def make_field(particles, sums, far_sums):
    sub, half = sums.shape[0] - 8, sums.shape[1]
    outs = [
        jax.ShapeDtypeStruct((sub, half), jnp.float32),
        jax.ShapeDtypeStruct((3 * sub // 4, sub), jnp.float32),
    ]
    return pl.pallas_call(
        functools.partial(field_kernel, 1.0 / particles),
        out_shape=outs,
        compiler_params=PARAMS,
        cost_estimate=pl.CostEstimate(
            flops=12 * sub * sub * half, bytes_accessed=2 * 2**20, transcendentals=0
        ),
        name="field",
    )(sums, far_sums)


def join_kernel(core_ref, own, other, upper, out, gram):
    sub = gram.shape[0]
    mid, low = sub // 2, sub // 4

    @pl.when(pl.program_id(0) == core_ref[0])
    def _():
        out[...] = own[...]

    @pl.when(pl.program_id(0) != core_ref[0])
    def _():
        out[...] = other[...]

    @pl.when(pl.program_id(0) == 0)
    def _():
        gram[:mid, :] = upper[:mid, :]
        last = jnp.concatenate([upper[mid:, :mid], upper[mid:, mid:]], axis=0)
        gram[mid:, :] = jnp.concatenate([upper[:mid, mid:].T, last], axis=1)


def join(core, own, other, upper):
    sub, half = own.shape
    outs = [
        jax.ShapeDtypeStruct((sub, 2 * half), jnp.float32),
        jax.ShapeDtypeStruct((sub, sub), jnp.float32),
    ]
    whole = lambda i, core: (0, 0)
    return pl.pallas_call(
        join_kernel,
        grid_spec=pltpu.PrefetchScalarGridSpec(
            num_scalar_prefetch=1,
            grid=(2,),
            in_specs=[pl.BlockSpec(x.shape, whole) for x in (own, other, upper)],
            out_specs=[
                pl.BlockSpec((sub, half), lambda i, core: (0, i)),
                pl.BlockSpec((sub, sub), whole),
            ],
        ),
        out_shape=outs,
        compiler_params=PARAMS,
        cost_estimate=pl.CostEstimate(flops=0, bytes_accessed=2 * 2**20, transcendentals=0),
        name="join",
    )(core, own, other, upper)


def swap(x):
    return lax.ppermute(x, "pair", [(0, 1), (1, 0)])


def shift(x, by):
    length = lax.axis_size("blk")
    return lax.ppermute(x, "blk", [(i, (i + by) % length) for i in range(length)])


def slot_of(distance):
    return distance + REACH - (distance > 0).astype(jnp.int32)


def per_device(features, subspace, offsets, counts):
    block = features.shape[0]
    core = lax.axis_index("pair").astype(jnp.int32).reshape(1)
    here = jnp.concatenate([slot_of(offsets), counts], axis=1)
    there = swap(here)
    packed = pack(core, features, subspace)
    up, down = [packed], [packed]
    for _ in range(REACH):
        up.append(shift(up[-1], 1))
        down.append(shift(down[-1], -1))
    near = [up[3], up[2], up[1], down[1], down[2], down[3]]
    own_sums, rows_t, row_norms = apply_self(core, features, packed)
    far = apply_partners("far", core, here, there, rows_t, row_norms, own_sums, near)
    far_sums = swap(far)
    sums = apply_partners("near", core, here, there, rows_t, row_norms, own_sums, near)
    field, upper = make_field(float(lax.axis_size("blk") * block), sums, far_sums)
    other = swap(field)
    return join(core, field, other, lax.psum(upper, ("blk", "pair")))


def solution(mesh):
    placed = (P("blk", None), P(None, "blk"), P("pair", "blk"), P("pair", "blk"))
    return jax.shard_map(
        per_device, mesh=mesh, in_specs=placed, out_specs=(P(None, "blk"), P()), check_vma=False
    )
```

```python
import functools

import jax
import jax.numpy as jnp
from jax import lax
from jax.experimental import pallas as pl
from jax.experimental.pallas import tpu as pltpu
from jax.sharding import PartitionSpec as P

REACH = 3
TILE = 256
FAR = 1e30
NT = (((1,), (1,)), ((), ()))
PARAMS = pltpu.CompilerParams(vmem_limit_bytes=32 * 2**20)


def pack_kernel(core_ref, feats_ref, field_ref, packed_ref, field_part, sems):
    half, feat = feats_ref.shape[0] // 2, feats_ref.shape[1]
    start = pl.multiple_of(core_ref[0] * half, half)
    feats_copy = pltpu.make_async_copy(
        feats_ref.at[pl.ds(start, half), :], packed_ref.at[pl.ds(0, half), :], sems.at[0]
    )
    field_copy = pltpu.make_async_copy(field_ref.at[:, pl.ds(start, half)], field_part, sems.at[1])
    feats_copy.start()
    field_copy.start()
    field_copy.wait()
    for at in range(0, half, feat):
        packed_ref[half + at : half + at + feat, :] = field_part[:, at : at + feat].astype(
            jnp.bfloat16
        )
    feats_copy.wait()


def pack(core, features, subspace):
    block, feat = features.shape
    sub = subspace.shape[0]
    return pl.pallas_call(
        pack_kernel,
        grid_spec=pltpu.PrefetchScalarGridSpec(
            num_scalar_prefetch=1,
            grid=(1,),
            in_specs=[pl.BlockSpec(memory_space=pltpu.HBM)] * 2,
            out_specs=pl.BlockSpec((block, feat), lambda i, core: (0, 0)),
            scratch_shapes=[
                pltpu.VMEM((sub, block // 2), jnp.float32),
                pltpu.SemaphoreType.DMA((2,)),
            ],
        ),
        out_shape=jax.ShapeDtypeStruct((block, feat), jnp.bfloat16),
        compiler_params=PARAMS,
        cost_estimate=pl.CostEstimate(flops=0, bytes_accessed=2 * 2**20, transcendentals=0),
        name="pack",
    )(core, features, subspace)


def norms_of(part):
    wide = part.astype(jnp.float32)
    return jnp.sum(wide * wide, axis=1, keepdims=True) * (1.0 / 256.0)


def add_columns(feats, vals, col_norms, rows_t, row_norms, sums, apart=None):
    sub = vals.shape[0]
    inner = jnp.dot(feats, rows_t, preferred_element_type=jnp.float32)
    weight = jnp.exp(inner - col_norms - row_norms)
    if apart is not None:
        weight = jnp.where(apart, weight, 0.0)
    sums[sub:, :] += jnp.sum(weight.reshape(TILE // 8, 8, weight.shape[1]), axis=0)
    sums[:sub, :] += jnp.dot(vals, weight.astype(jnp.bfloat16), preferred_element_type=jnp.float32)


def values_at(held, start):
    first = held[pl.ds(pl.multiple_of(start, 128), 128), :]
    second = held[pl.ds(pl.multiple_of(start + 128, 128), 128), :]
    return jnp.concatenate([first, second], axis=1)


def self_kernel(core_ref, feats_ref, packed, sums, rows_t, row_norms, feats, sem):
    block = feats_ref.shape[0]
    half = block // 2
    copy = pltpu.make_async_copy(feats_ref, feats, sem)
    copy.start()
    sums[...] = jnp.zeros_like(sums)
    copy.wait()
    for at in range(0, block, TILE):
        wide = feats[at : at + TILE, :].astype(jnp.float32).T
        row_norms[:, at : at + TILE] = jnp.sum(wide * wide, axis=0, keepdims=True) * (1.0 / 256.0)
        rows_t[:, at : at + TILE] = (wide * (1.0 / 128.0)).astype(jnp.bfloat16)

    @pl.loop(0, half // TILE)
    def _(step):
        at = pl.multiple_of(step * TILE, TILE)
        part = packed[pl.ds(at, TILE), :]
        col_ids = core_ref[0] * half + at + lax.broadcasted_iota(jnp.int32, (TILE, block), 0)
        row_ids = lax.broadcasted_iota(jnp.int32, (TILE, block), 1)
        add_columns(
            part,
            values_at(packed, half + at),
            norms_of(part),
            rows_t[...],
            row_norms[...],
            sums,
            col_ids != row_ids,
        )


def apply_self(core, features, packed):
    block, feat = features.shape
    outs = [
        jax.ShapeDtypeStruct((feat + 8, block), jnp.float32),
        jax.ShapeDtypeStruct((feat, block), jnp.bfloat16),
        jax.ShapeDtypeStruct((1, block), jnp.float32),
    ]
    whole = lambda i, core: (0, 0)
    return pl.pallas_call(
        self_kernel,
        grid_spec=pltpu.PrefetchScalarGridSpec(
            num_scalar_prefetch=1,
            grid=(1,),
            in_specs=[pl.BlockSpec(memory_space=pltpu.HBM), pl.BlockSpec(packed.shape, whole)],
            out_specs=[pl.BlockSpec(x.shape, whole) for x in outs],
            scratch_shapes=[pltpu.VMEM((block, feat), jnp.bfloat16), pltpu.SemaphoreType.DMA],
        ),
        out_shape=outs,
        compiler_params=PARAMS,
        cost_estimate=pl.CostEstimate(
            flops=2 * 2 * block * block // 2 * feat,
            bytes_accessed=4 * 2**20,
            transcendentals=block * block // 2,
        ),
        name="own_block",
    )(core, features, packed)


def partner_kernel(core_ref, here, there, rows_t, row_norms, own_sums, *refs):
    near = refs[: 2 * REACH]
    sums, held, sems = refs[2 * REACH :]
    half = held.shape[1] // 2
    picks = (here, there)
    for turn in range(2):
        for slot in range(2 * REACH):

            @pl.when(picks[turn][0, 0] == slot)
            def _():
                pltpu.make_async_copy(near[slot], held.at[turn], sems.at[turn]).start()

    sums[...] = own_sums[...]
    for turn in range(2):
        pltpu.make_async_copy(near[0], held.at[turn], sems.at[turn]).wait()

        @pl.loop(0, half // TILE)
        def _(step):
            at = pl.multiple_of(step * TILE, TILE)
            part = held[turn, pl.ds(at, TILE), :]
            ids = core_ref[0] * half + at + lax.broadcasted_iota(jnp.int32, (TILE, 1), 0)
            norms = jnp.where(ids < picks[turn][0, 1], norms_of(part), FAR)
            vals = values_at(held.at[turn], half + at)
            add_columns(part, vals, norms, rows_t[...], row_norms[...], sums)


def apply_partners(which, core, here, there, rows_t, row_norms, own_sums, near):
    feat, block = rows_t.shape
    half = block // 2
    if which == "far":
        picked = lambda i, core, here, there: (0, 1 - core[0])
    else:
        picked = lambda i, core, here, there: (0, core[0])
    out = jax.ShapeDtypeStruct((feat + 8, half), jnp.float32)
    return pl.pallas_call(
        partner_kernel,
        grid_spec=pltpu.PrefetchScalarGridSpec(
            num_scalar_prefetch=3,
            grid=(1,),
            in_specs=[
                pl.BlockSpec((feat, half), picked),
                pl.BlockSpec((1, half), picked),
                pl.BlockSpec((feat + 8, half), picked),
            ]
            + [pl.BlockSpec(memory_space=pl.ANY)] * len(near),
            out_specs=pl.BlockSpec(out.shape, lambda i, core, here, there: (0, 0)),
            scratch_shapes=[
                pltpu.VMEM((2, *near[0].shape), jnp.bfloat16),
                pltpu.SemaphoreType.DMA((2,)),
            ],
        ),
        out_shape=out,
        compiler_params=PARAMS,
        cost_estimate=pl.CostEstimate(
            flops=2 * 2 * half * block * feat,
            bytes_accessed=3 * 2**20,
            transcendentals=half * block,
        ),
        name="partners_" + which,
    )(core, here, there, rows_t, row_norms, own_sums, *near)


def field_kernel(scale, sums, far_sums, field, gram):
    sub = field.shape[0]
    degree = jnp.sum(sums[sub:, :] + far_sums[sub:, :], axis=0, keepdims=True)
    field[...] = (sums[:sub, :] + far_sums[:sub, :]) / degree
    terms = lax.dot_general(
        field[...],
        field[...],
        NT,
        precision=lax.Precision.HIGHEST,
        preferred_element_type=jnp.float32,
    )
    gram[...] = (terms * scale).reshape(gram.shape)


def make_field(particles, sums, far_sums):
    sub, half = sums.shape[0] - 8, sums.shape[1]
    outs = [
        jax.ShapeDtypeStruct((sub, half), jnp.float32),
        jax.ShapeDtypeStruct((sub // 8, 8, sub), jnp.float32),
    ]
    return pl.pallas_call(
        functools.partial(field_kernel, 1.0 / particles),
        out_shape=outs,
        compiler_params=PARAMS,
        cost_estimate=pl.CostEstimate(
            flops=12 * sub * sub * half, bytes_accessed=2 * 2**20, transcendentals=0
        ),
        name="field",
    )(sums, far_sums)


def join_kernel(core_ref, own, other, out):
    @pl.when(pl.program_id(0) == core_ref[0])
    def _():
        out[...] = own[...]

    @pl.when(pl.program_id(0) != core_ref[0])
    def _():
        out[...] = other[...]


def join(core, own, other):
    sub, half = own.shape
    return pl.pallas_call(
        join_kernel,
        grid_spec=pltpu.PrefetchScalarGridSpec(
            num_scalar_prefetch=1,
            grid=(2,),
            in_specs=[pl.BlockSpec((sub, half), lambda i, core: (0, 0))] * 2,
            out_specs=pl.BlockSpec((sub, half), lambda i, core: (0, i)),
        ),
        out_shape=jax.ShapeDtypeStruct((sub, 2 * half), jnp.float32),
        compiler_params=PARAMS,
        cost_estimate=pl.CostEstimate(flops=0, bytes_accessed=2 * 2**20, transcendentals=0),
        name="join",
    )(core, own, other)


def exchange(tiles, groups):
    return lax.all_to_all(tiles, "blk", 0, 0, axis_index_groups=groups, tiled=True)


def sum_over_all(tiles):
    count = tiles.shape[0]
    blocks = lax.axis_size("blk")
    near_z = [list(range(i, i + count)) for i in range(0, blocks, count)]
    planes = [list(range(i, blocks, count)) for i in range(count)]
    part = jnp.sum(exchange(tiles, planes), axis=0)
    part = part + swap(part)
    part = jnp.sum(exchange(jnp.broadcast_to(part, tiles.shape), near_z), axis=0)
    return exchange(jnp.broadcast_to(part, tiles.shape), planes)


def swap(x):
    return lax.ppermute(x, "pair", [(0, 1), (1, 0)])


def shift(x, by):
    length = lax.axis_size("blk")
    return lax.ppermute(x, "blk", [(i, (i + by) % length) for i in range(length)])


def slot_of(distance):
    return distance + REACH - (distance > 0).astype(jnp.int32)


def per_device(features, subspace, offsets, counts):
    block = features.shape[0]
    core = lax.axis_index("pair").astype(jnp.int32).reshape(1)
    here = jnp.concatenate([slot_of(offsets), counts], axis=1)
    there = swap(here)
    packed = pack(core, features, subspace)
    up, down = [packed], [packed]
    for _ in range(REACH):
        up.append(shift(up[-1], 1))
        down.append(shift(down[-1], -1))
    near = [up[3], up[2], up[1], down[1], down[2], down[3]]
    own_sums, rows_t, row_norms = apply_self(core, features, packed)
    far = apply_partners("far", core, here, there, rows_t, row_norms, own_sums, near)
    far_sums = swap(far)
    sums = apply_partners("near", core, here, there, rows_t, row_norms, own_sums, near)
    field, tiles = make_field(float(lax.axis_size("blk") * block), sums, far_sums)
    other = swap(field)
    sub = field.shape[0]
    return (join(core, field, other), sum_over_all(tiles).reshape(sub, sub))


def solution(mesh):
    placed = (P("blk", None), P(None, "blk"), P("pair", "blk"), P("pair", "blk"))
    return jax.shard_map(
        per_device, mesh=mesh, in_specs=placed, out_specs=(P(None, "blk"), P()), check_vma=False
    )
```

```python
import functools

import jax
import jax.numpy as jnp
from jax import lax
from jax.experimental import pallas as pl
from jax.experimental.pallas import tpu as pltpu
from jax.sharding import PartitionSpec as P

REACH = 3
SIDE = 4
LENGTH = 16
TILE = 256
FAR = 1e30
NT = (((1,), (1,)), ((), ()))
PARAMS = pltpu.CompilerParams(vmem_limit_bytes=32 * 2**20)


def pack_kernel(core_ref, feats_ref, field_ref, give, keep):
    half, feat = feats_ref.shape[0] // 2, feats_ref.shape[1]
    for core in range(2):

        @pl.when(core_ref[0] == core)
        def _():
            for packed, start in ((give, (1 - core) * half), (keep, core * half)):
                packed[:half, :] = feats_ref[start : start + half, :]
                for at in range(0, half, feat):
                    packed[half + at : half + at + feat, :] = field_ref[
                        :, start + at : start + at + feat
                    ].astype(jnp.bfloat16)


def pack(core, features, subspace):
    out = jax.ShapeDtypeStruct(features.shape, jnp.bfloat16)
    whole = lambda i, core: (0, 0)
    return pl.pallas_call(
        pack_kernel,
        grid_spec=pltpu.PrefetchScalarGridSpec(
            num_scalar_prefetch=1,
            grid=(1,),
            in_specs=[pl.BlockSpec(x.shape, whole) for x in (features, subspace)],
            out_specs=[pl.BlockSpec(out.shape, whole)] * 2,
        ),
        out_shape=[out, out],
        compiler_params=PARAMS,
        cost_estimate=pl.CostEstimate(flops=0, bytes_accessed=2 * 2**20, transcendentals=0),
        name="pack",
    )(core, features, subspace)


def norms_of(part):
    wide = part.astype(jnp.float32)
    return jnp.sum(wide * wide, axis=1, keepdims=True) * (1.0 / 256.0)


def add_columns(feats, vals, col_norms, rows_t, row_norms, sums, apart=None):
    sub = vals.shape[0]
    inner = jnp.dot(feats, rows_t, preferred_element_type=jnp.float32)
    weight = jnp.exp(inner - col_norms - row_norms)
    if apart is not None:
        weight = jnp.where(apart, weight, 0.0)
    sums[sub:, :] += jnp.sum(weight.reshape(TILE // 8, 8, weight.shape[1]), axis=0)
    sums[:sub, :] += jnp.dot(vals, weight.astype(jnp.bfloat16), preferred_element_type=jnp.float32)


def values_at(held, start):
    first = held[pl.ds(pl.multiple_of(start, 128), 128), :]
    second = held[pl.ds(pl.multiple_of(start + 128, 128), 128), :]
    return jnp.concatenate([first, second], axis=1)


def self_kernel(core_ref, feats_ref, packed, sums, rows_t, row_norms, feats, sem):
    block = feats_ref.shape[0]
    half = block // 2
    copy = pltpu.make_async_copy(feats_ref, feats, sem)
    copy.start()
    sums[...] = jnp.zeros_like(sums)
    copy.wait()
    for at in range(0, block, TILE):
        wide = feats[at : at + TILE, :].astype(jnp.float32).T
        row_norms[:, at : at + TILE] = jnp.sum(wide * wide, axis=0, keepdims=True) * (1.0 / 256.0)
        rows_t[:, at : at + TILE] = (wide * (1.0 / 128.0)).astype(jnp.bfloat16)

    @pl.loop(0, half // TILE)
    def _(step):
        at = pl.multiple_of(step * TILE, TILE)
        part = packed[pl.ds(at, TILE), :]
        col_ids = core_ref[0] * half + at + lax.broadcasted_iota(jnp.int32, (TILE, block), 0)
        row_ids = lax.broadcasted_iota(jnp.int32, (TILE, block), 1)
        add_columns(
            part,
            values_at(packed, half + at),
            norms_of(part),
            rows_t[...],
            row_norms[...],
            sums,
            col_ids != row_ids,
        )


def apply_self(core, features, packed):
    block, feat = features.shape
    outs = [
        jax.ShapeDtypeStruct((feat + 8, block), jnp.float32),
        jax.ShapeDtypeStruct((feat, block), jnp.bfloat16),
        jax.ShapeDtypeStruct((1, block), jnp.float32),
    ]
    whole = lambda i, core: (0, 0)
    return pl.pallas_call(
        self_kernel,
        grid_spec=pltpu.PrefetchScalarGridSpec(
            num_scalar_prefetch=1,
            grid=(1,),
            in_specs=[pl.BlockSpec(memory_space=pltpu.HBM), pl.BlockSpec(packed.shape, whole)],
            out_specs=[pl.BlockSpec(x.shape, whole) for x in outs],
            scratch_shapes=[pltpu.VMEM((block, feat), jnp.bfloat16), pltpu.SemaphoreType.DMA],
        ),
        out_shape=outs,
        compiler_params=PARAMS,
        cost_estimate=pl.CostEstimate(
            flops=2 * 2 * block * block // 2 * feat,
            bytes_accessed=4 * 2**20,
            transcendentals=block * block // 2,
        ),
        name="own_block",
    )(core, features, packed)


def partner_kernel(core_ref, here, there, rows_t, row_norms, own_sums, *refs):
    near = refs[: 2 * REACH]
    sums, held, sems = refs[2 * REACH :]
    half = held.shape[1] // 2
    picks = (here, there)
    for turn in range(2):
        distance = picks[turn][0, 0]
        same_way = (distance < 0) == (core_ref[0] == 0)
        chosen = jnp.abs(distance) - 1 + jnp.where(same_way, 0, REACH)
        for slot in range(2 * REACH):

            @pl.when(chosen == slot)
            def _():
                pltpu.make_async_copy(near[slot], held.at[turn], sems.at[turn]).start()

    sums[...] = own_sums[...]
    for turn in range(2):
        pltpu.make_async_copy(near[0], held.at[turn], sems.at[turn]).wait()

        @pl.loop(0, half // TILE, unroll=True)
        def _(step):
            at = pl.multiple_of(step * TILE, TILE)
            part = held[turn, pl.ds(at, TILE), :]
            ids = core_ref[0] * half + at + lax.broadcasted_iota(jnp.int32, (TILE, 1), 0)
            norms = jnp.where(ids < picks[turn][0, 1], norms_of(part), FAR)
            vals = values_at(held.at[turn], half + at)
            add_columns(part, vals, norms, rows_t[...], row_norms[...], sums)


def apply_partners(which, core, here, there, rows_t, row_norms, own_sums, near):
    feat, block = rows_t.shape
    half = block // 2
    if which == "far":
        picked = lambda i, core, here, there: (0, 1 - core[0])
    else:
        picked = lambda i, core, here, there: (0, core[0])
    out = jax.ShapeDtypeStruct((feat + 8, half), jnp.float32)
    return pl.pallas_call(
        partner_kernel,
        grid_spec=pltpu.PrefetchScalarGridSpec(
            num_scalar_prefetch=3,
            grid=(1,),
            in_specs=[
                pl.BlockSpec((feat, half), picked),
                pl.BlockSpec((1, half), picked),
                pl.BlockSpec((feat + 8, half), picked),
            ]
            + [pl.BlockSpec(memory_space=pl.ANY)] * len(near),
            out_specs=pl.BlockSpec(out.shape, lambda i, core, here, there: (0, 0)),
            scratch_shapes=[
                pltpu.VMEM((2, *near[0].shape), jnp.bfloat16),
                pltpu.SemaphoreType.DMA((2,)),
            ],
        ),
        out_shape=out,
        compiler_params=PARAMS,
        cost_estimate=pl.CostEstimate(
            flops=2 * 2 * half * block * feat,
            bytes_accessed=3 * 2**20,
            transcendentals=half * block,
        ),
        name="partners_" + which,
    )(core, here, there, rows_t, row_norms, own_sums, *near)


def field_kernel(scale, sums, far_sums, field, gram):
    sub = field.shape[0]
    degree = jnp.sum(sums[sub:, :] + far_sums[sub:, :], axis=0, keepdims=True)
    field[...] = (sums[:sub, :] + far_sums[:sub, :]) / degree
    terms = lax.dot_general(
        field[...],
        field[...],
        NT,
        precision=lax.Precision.HIGHEST,
        preferred_element_type=jnp.float32,
    )
    gram[...] = terms * scale


def make_field(particles, sums, far_sums):
    sub, half = sums.shape[0] - 8, sums.shape[1]
    outs = [
        jax.ShapeDtypeStruct((sub, half), jnp.float32),
        jax.ShapeDtypeStruct((sub, sub), jnp.float32),
    ]
    return pl.pallas_call(
        functools.partial(field_kernel, 1.0 / particles),
        out_shape=outs,
        compiler_params=PARAMS,
        cost_estimate=pl.CostEstimate(
            flops=12 * sub * sub * half, bytes_accessed=2 * 2**20, transcendentals=0
        ),
        name="field",
    )(sums, far_sums)


def join_kernel(core_ref, own, other, out):
    @pl.when(pl.program_id(0) == core_ref[0])
    def _():
        out[...] = own[...]

    @pl.when(pl.program_id(0) != core_ref[0])
    def _():
        out[...] = other[...]


def join(core, own, other):
    sub, half = own.shape
    return pl.pallas_call(
        join_kernel,
        grid_spec=pltpu.PrefetchScalarGridSpec(
            num_scalar_prefetch=1,
            grid=(2,),
            in_specs=[pl.BlockSpec((sub, half), lambda i, core: (0, 0))] * 2,
            out_specs=pl.BlockSpec((sub, half), lambda i, core: (0, i)),
        ),
        out_shape=jax.ShapeDtypeStruct((sub, 2 * half), jnp.float32),
        compiler_params=PARAMS,
        cost_estimate=pl.CostEstimate(flops=0, bytes_accessed=2 * 2**20, transcendentals=0),
        name="join",
    )(core, own, other)


def exchange(pieces, stride):
    count = pieces.shape[0]
    blocks = lax.axis_size("blk")
    groups = [
        list(range(start, start + count * stride, stride))
        for start in range(blocks)
        if start // stride % count == 0
    ]
    return lax.all_to_all(pieces, "blk", 0, 0, axis_index_groups=groups, tiled=True)


def repeat(piece):
    return jnp.broadcast_to(piece, (SIDE, *piece.shape))


def sum_over_all(gram):
    size = gram.shape[0]
    part = gram.reshape(SIDE, size // SIDE, size)
    part = jnp.sum(exchange(part, LENGTH), axis=0)
    part = part.reshape(SIDE, size // SIDE // SIDE, size)
    part = jnp.sum(exchange(part, LENGTH * SIDE), axis=0)
    part = part + swap(part)
    part = jnp.sum(exchange(repeat(part), 1), axis=0)
    part = jnp.sum(exchange(repeat(part), SIDE), axis=0)
    part = exchange(repeat(part), LENGTH * SIDE).reshape(size // SIDE, size)
    return exchange(repeat(part), LENGTH).reshape(size, size)


def swap(x):
    return lax.ppermute(x, "pair", [(0, 1), (1, 0)])


def relay(x):
    blocks = lax.axis_size("blk")
    pairs = []
    for i in range(blocks):
        pairs.append((2 * i, (i + 1) % blocks * 2))
        pairs.append((2 * i + 1, (i - 1) % blocks * 2 + 1))
    return lax.ppermute(x, ("blk", "pair"), pairs)


def per_device(features, subspace, offsets, counts):
    block = features.shape[0]
    core = lax.axis_index("pair").astype(jnp.int32).reshape(1)
    here = jnp.concatenate([offsets, counts], axis=1)
    there = swap(here)
    give, keep = pack(core, features, subspace)
    own_sums, rows_t, row_norms = apply_self(core, features, keep)
    kept, swapped = [], []
    for _ in range(REACH):
        give, keep = relay(give), relay(keep)
        kept.append(keep)
        swapped.append(swap(give))
    near = kept + swapped
    far = apply_partners("far", core, here, there, rows_t, row_norms, own_sums, near)
    far_sums = swap(far)
    sums = apply_partners("near", core, here, there, rows_t, row_norms, own_sums, near)
    field, gram = make_field(float(lax.axis_size("blk") * block), sums, far_sums)
    other = swap(field)
    return (join(core, field, other), sum_over_all(gram))


def solution(mesh):
    placed = (P("blk", None), P(None, "blk"), P("pair", "blk"), P("pair", "blk"))
    return jax.shard_map(
        per_device, mesh=mesh, in_specs=placed, out_specs=(P(None, "blk"), P()), check_vma=False
    )
```

```python
import functools

import jax
import jax.numpy as jnp
from jax import lax
from jax.experimental import pallas as pl
from jax.experimental.pallas import tpu as pltpu
from jax.sharding import PartitionSpec as P

REACH = 3
TILE = 256
FAR = 1e30
NT = (((1,), (1,)), ((), ()))
PARAMS = pltpu.CompilerParams(vmem_limit_bytes=32 * 2**20)


def pack_kernel(core_ref, feats_ref, field_ref, give, keep):
    half, feat = feats_ref.shape[0] // 2, feats_ref.shape[1]
    for core in range(2):

        @pl.when(core_ref[0] == core)
        def _():
            for packed, start in ((give, (1 - core) * half), (keep, core * half)):
                packed[:half, :] = feats_ref[start : start + half, :]
                for at in range(0, half, feat):
                    packed[half + at : half + at + feat, :] = field_ref[
                        :, start + at : start + at + feat
                    ].astype(jnp.bfloat16)


def pack(core, features, subspace):
    out = jax.ShapeDtypeStruct(features.shape, jnp.bfloat16)
    whole = lambda i, core: (0, 0)
    return pl.pallas_call(
        pack_kernel,
        grid_spec=pltpu.PrefetchScalarGridSpec(
            num_scalar_prefetch=1,
            grid=(1,),
            in_specs=[pl.BlockSpec(x.shape, whole) for x in (features, subspace)],
            out_specs=[pl.BlockSpec(out.shape, whole)] * 2,
        ),
        out_shape=[out, out],
        compiler_params=PARAMS,
        cost_estimate=pl.CostEstimate(flops=0, bytes_accessed=2 * 2**20, transcendentals=0),
        name="pack",
    )(core, features, subspace)


def norms_of(part):
    wide = part.astype(jnp.float32)
    return jnp.sum(wide * wide, axis=1, keepdims=True) * (1.0 / 256.0)


def add_columns(feats, vals, col_norms, rows_t, row_norms, sums, apart=None):
    sub = vals.shape[0]
    inner = jnp.dot(feats, rows_t, preferred_element_type=jnp.float32)
    weight = jnp.exp(inner - col_norms - row_norms)
    if apart is not None:
        weight = jnp.where(apart, weight, 0.0)
    sums[sub:, :] += jnp.sum(weight.reshape(TILE // 8, 8, weight.shape[1]), axis=0)
    sums[:sub, :] += jnp.dot(vals, weight.astype(jnp.bfloat16), preferred_element_type=jnp.float32)


def values_at(held, start):
    first = held[pl.ds(pl.multiple_of(start, 128), 128), :]
    second = held[pl.ds(pl.multiple_of(start + 128, 128), 128), :]
    return jnp.concatenate([first, second], axis=1)


def self_kernel(core_ref, feats_ref, packed, sums, rows_t, row_norms, feats, sem):
    block = feats_ref.shape[0]
    half = block // 2
    copy = pltpu.make_async_copy(feats_ref, feats, sem)
    copy.start()
    sums[...] = jnp.zeros_like(sums)
    copy.wait()
    for at in range(0, block, TILE):
        wide = feats[at : at + TILE, :].astype(jnp.float32).T
        row_norms[:, at : at + TILE] = jnp.sum(wide * wide, axis=0, keepdims=True) * (1.0 / 256.0)
        rows_t[:, at : at + TILE] = (wide * (1.0 / 128.0)).astype(jnp.bfloat16)

    @pl.loop(0, half // TILE)
    def _(step):
        at = pl.multiple_of(step * TILE, TILE)
        part = packed[pl.ds(at, TILE), :]
        col_ids = core_ref[0] * half + at + lax.broadcasted_iota(jnp.int32, (TILE, block), 0)
        row_ids = lax.broadcasted_iota(jnp.int32, (TILE, block), 1)
        add_columns(
            part,
            values_at(packed, half + at),
            norms_of(part),
            rows_t[...],
            row_norms[...],
            sums,
            col_ids != row_ids,
        )


def apply_self(core, features, packed):
    block, feat = features.shape
    outs = [
        jax.ShapeDtypeStruct((feat + 8, block), jnp.float32),
        jax.ShapeDtypeStruct((feat, block), jnp.bfloat16),
        jax.ShapeDtypeStruct((1, block), jnp.float32),
    ]
    whole = lambda i, core: (0, 0)
    return pl.pallas_call(
        self_kernel,
        grid_spec=pltpu.PrefetchScalarGridSpec(
            num_scalar_prefetch=1,
            grid=(1,),
            in_specs=[pl.BlockSpec(memory_space=pltpu.HBM), pl.BlockSpec(packed.shape, whole)],
            out_specs=[pl.BlockSpec(x.shape, whole) for x in outs],
            scratch_shapes=[pltpu.VMEM((block, feat), jnp.bfloat16), pltpu.SemaphoreType.DMA],
        ),
        out_shape=outs,
        compiler_params=PARAMS,
        cost_estimate=pl.CostEstimate(
            flops=2 * 2 * block * block // 2 * feat,
            bytes_accessed=4 * 2**20,
            transcendentals=block * block // 2,
        ),
        name="own_block",
    )(core, features, packed)


def partner_kernel(core_ref, here, there, rows_t, row_norms, own_sums, *refs):
    near = refs[: 2 * REACH]
    sums, held, sems = refs[2 * REACH :]
    half = held.shape[1] // 2
    picks = (here, there)
    for turn in range(2):
        distance = picks[turn][0, 0]
        same_way = (distance < 0) == (core_ref[0] == 0)
        chosen = jnp.abs(distance) - 1 + jnp.where(same_way, 0, REACH)
        for slot in range(2 * REACH):

            @pl.when(chosen == slot)
            def _():
                pltpu.make_async_copy(near[slot], held.at[turn], sems.at[turn]).start()

    sums[...] = own_sums[...]
    for turn in range(2):
        pltpu.make_async_copy(near[0], held.at[turn], sems.at[turn]).wait()

        @pl.loop(0, half // TILE, unroll=True)
        def _(step):
            at = pl.multiple_of(step * TILE, TILE)
            part = held[turn, pl.ds(at, TILE), :]
            ids = core_ref[0] * half + at + lax.broadcasted_iota(jnp.int32, (TILE, 1), 0)
            norms = jnp.where(ids < picks[turn][0, 1], norms_of(part), FAR)
            vals = values_at(held.at[turn], half + at)
            add_columns(part, vals, norms, rows_t[...], row_norms[...], sums)


def apply_partners(which, core, here, there, rows_t, row_norms, own_sums, near):
    feat, block = rows_t.shape
    half = block // 2
    if which == "far":
        picked = lambda i, core, here, there: (0, 1 - core[0])
    else:
        picked = lambda i, core, here, there: (0, core[0])
    out = jax.ShapeDtypeStruct((feat + 8, half), jnp.float32)
    return pl.pallas_call(
        partner_kernel,
        grid_spec=pltpu.PrefetchScalarGridSpec(
            num_scalar_prefetch=3,
            grid=(1,),
            in_specs=[
                pl.BlockSpec((feat, half), picked),
                pl.BlockSpec((1, half), picked),
                pl.BlockSpec((feat + 8, half), picked),
            ]
            + [pl.BlockSpec(memory_space=pl.ANY)] * len(near),
            out_specs=pl.BlockSpec(out.shape, lambda i, core, here, there: (0, 0)),
            scratch_shapes=[
                pltpu.VMEM((2, *near[0].shape), jnp.bfloat16),
                pltpu.SemaphoreType.DMA((2,)),
            ],
        ),
        out_shape=out,
        compiler_params=PARAMS,
        cost_estimate=pl.CostEstimate(
            flops=2 * 2 * half * block * feat,
            bytes_accessed=3 * 2**20,
            transcendentals=half * block,
        ),
        name="partners_" + which,
    )(core, here, there, rows_t, row_norms, own_sums, *near)


def field_kernel(scale, sums, far_sums, field, gram):
    sub = field.shape[0]
    degree = jnp.sum(sums[sub:, :] + far_sums[sub:, :], axis=0, keepdims=True)
    field[...] = (sums[:sub, :] + far_sums[:sub, :]) / degree
    terms = lax.dot_general(
        field[...],
        field[...],
        NT,
        precision=lax.Precision.HIGHEST,
        preferred_element_type=jnp.float32,
    )
    gram[...] = (terms * scale).reshape(gram.shape)


def make_field(particles, sums, far_sums):
    sub, half = sums.shape[0] - 8, sums.shape[1]
    outs = [
        jax.ShapeDtypeStruct((sub, half), jnp.float32),
        jax.ShapeDtypeStruct((sub // 8, 8, sub), jnp.float32),
    ]
    return pl.pallas_call(
        functools.partial(field_kernel, 1.0 / particles),
        out_shape=outs,
        compiler_params=PARAMS,
        cost_estimate=pl.CostEstimate(
            flops=12 * sub * sub * half, bytes_accessed=2 * 2**20, transcendentals=0
        ),
        name="field",
    )(sums, far_sums)


def join_kernel(core_ref, own, other, tiles, out, gram):
    @pl.when(pl.program_id(0) == core_ref[0])
    def _():
        out[...] = own[...]

    @pl.when(pl.program_id(0) != core_ref[0])
    def _():
        out[...] = other[...]

    @pl.when(pl.program_id(0) == 0)
    def _():
        gram[...] = tiles[...].reshape(gram.shape)


def join(core, own, other, tiles):
    sub, half = own.shape
    outs = [
        jax.ShapeDtypeStruct((sub, 2 * half), jnp.float32),
        jax.ShapeDtypeStruct((sub, sub), jnp.float32),
    ]
    return pl.pallas_call(
        join_kernel,
        grid_spec=pltpu.PrefetchScalarGridSpec(
            num_scalar_prefetch=1,
            grid=(2,),
            in_specs=[pl.BlockSpec((sub, half), lambda i, core: (0, 0))] * 2
            + [pl.BlockSpec(tiles.shape, lambda i, core: (0, 0, 0))],
            out_specs=[
                pl.BlockSpec((sub, half), lambda i, core: (0, i)),
                pl.BlockSpec((sub, sub), lambda i, core: (0, 0)),
            ],
        ),
        out_shape=outs,
        compiler_params=PARAMS,
        cost_estimate=pl.CostEstimate(flops=0, bytes_accessed=2 * 2**20, transcendentals=0),
        name="join",
    )(core, own, other, tiles)


def exchange(tiles, groups):
    return lax.all_to_all(tiles, "blk", 0, 0, axis_index_groups=groups, tiled=True)


def sum_over_all(tiles):
    count = tiles.shape[0]
    blocks = lax.axis_size("blk")
    near_z = [list(range(i, i + count)) for i in range(0, blocks, count)]
    planes = [list(range(i, blocks, count)) for i in range(count)]
    part = jnp.sum(exchange(tiles, planes), axis=0)
    part = part + swap(part)
    part = jnp.sum(exchange(jnp.broadcast_to(part, tiles.shape), near_z), axis=0)
    return exchange(jnp.broadcast_to(part, tiles.shape), planes)


def swap(x):
    return lax.ppermute(x, "pair", [(0, 1), (1, 0)])


def relay(x):
    blocks = lax.axis_size("blk")
    pairs = []
    for i in range(blocks):
        pairs.append((2 * i, (i + 1) % blocks * 2))
        pairs.append((2 * i + 1, (i - 1) % blocks * 2 + 1))
    return lax.ppermute(x, ("blk", "pair"), pairs)


def per_device(features, subspace, offsets, counts):
    block = features.shape[0]
    core = lax.axis_index("pair").astype(jnp.int32).reshape(1)
    here = jnp.concatenate([offsets, counts], axis=1)
    there = swap(here)
    give, keep = pack(core, features, subspace)
    own_sums, rows_t, row_norms = apply_self(core, features, keep)
    kept, swapped = [], []
    for step in range(REACH):
        give, keep = relay(give), relay(keep)
        if step == 0:
            give, there, own_sums, rows_t, row_norms = lax.optimization_barrier(
                (give, there, own_sums, rows_t, row_norms)
            )
        kept.append(keep)
        swapped.append(swap(give))
    near = kept + swapped
    far = apply_partners("far", core, here, there, rows_t, row_norms, own_sums, near)
    far_sums = swap(far)
    sums = apply_partners("near", core, here, there, rows_t, row_norms, own_sums, near)
    field, gram = make_field(float(lax.axis_size("blk") * block), sums, far_sums)
    other = swap(field)
    return tuple(join(core, field, other, sum_over_all(gram)))


def solution(mesh):
    placed = (P("blk", None), P(None, "blk"), P("pair", "blk"), P("pair", "blk"))
    return jax.shard_map(
        per_device, mesh=mesh, in_specs=placed, out_specs=(P(None, "blk"), P()), check_vma=False
    )
```

```python
import functools

import jax
import jax.numpy as jnp
from jax import lax
from jax.experimental import pallas as pl
from jax.experimental.pallas import tpu as pltpu
from jax.sharding import PartitionSpec as P

REACH = 3
TILE = 256
FAR = 1e30
NT = (((1,), (1,)), ((), ()))
PARAMS = pltpu.CompilerParams(vmem_limit_bytes=32 * 2**20)


def pack_kernel(core_ref, feats_ref, field_ref, give, keep):
    half, feat = feats_ref.shape[0] // 2, feats_ref.shape[1]
    for core in range(2):

        @pl.when(core_ref[0] == core)
        def _():
            for packed, start in ((give, (1 - core) * half), (keep, core * half)):
                packed[:half, :] = feats_ref[start : start + half, :]
                for at in range(0, half, feat):
                    packed[half + at : half + at + feat, :] = field_ref[
                        :, start + at : start + at + feat
                    ].astype(jnp.bfloat16)


def pack(core, features, subspace):
    out = jax.ShapeDtypeStruct(features.shape, jnp.bfloat16)
    whole = lambda i, core: (0, 0)
    return pl.pallas_call(
        pack_kernel,
        grid_spec=pltpu.PrefetchScalarGridSpec(
            num_scalar_prefetch=1,
            grid=(1,),
            in_specs=[pl.BlockSpec(x.shape, whole) for x in (features, subspace)],
            out_specs=[pl.BlockSpec(out.shape, whole)] * 2,
        ),
        out_shape=[out, out],
        compiler_params=pltpu.CompilerParams(vmem_limit_bytes=62 * 2**20),
        cost_estimate=pl.CostEstimate(flops=0, bytes_accessed=2 * 2**20, transcendentals=0),
        name="pack",
    )(core, features, subspace)


def norms_of(part):
    wide = part.astype(jnp.float32)
    return jnp.sum(wide * wide, axis=1, keepdims=True) * (1.0 / 256.0)


def add_columns(feats, vals, col_norms, rows_t, row_norms, sums, apart=None):
    sub = vals.shape[0]
    inner = jnp.dot(feats, rows_t, preferred_element_type=jnp.float32)
    weight = jnp.exp(inner - col_norms - row_norms)
    if apart is not None:
        weight = jnp.where(apart, weight, 0.0)
    sums[sub:, :] += jnp.sum(weight.reshape(TILE // 8, 8, weight.shape[1]), axis=0)
    sums[:sub, :] += jnp.dot(vals, weight.astype(jnp.bfloat16), preferred_element_type=jnp.float32)


def values_at(held, start):
    first = held[pl.ds(pl.multiple_of(start, 128), 128), :]
    second = held[pl.ds(pl.multiple_of(start + 128, 128), 128), :]
    return jnp.concatenate([first, second], axis=1)


def self_kernel(core_ref, feats_ref, packed, sums, rows_t, row_norms, feats, sem):
    block = feats_ref.shape[0]
    half = block // 2
    copy = pltpu.make_async_copy(feats_ref, feats, sem)
    copy.start()
    sums[...] = jnp.zeros_like(sums)
    copy.wait()
    for at in range(0, block, TILE):
        wide = feats[at : at + TILE, :].astype(jnp.float32).T
        row_norms[:, at : at + TILE] = jnp.sum(wide * wide, axis=0, keepdims=True) * (1.0 / 256.0)
        rows_t[:, at : at + TILE] = (wide * (1.0 / 128.0)).astype(jnp.bfloat16)

    @pl.loop(0, half // TILE)
    def _(step):
        at = pl.multiple_of(step * TILE, TILE)
        part = packed[pl.ds(at, TILE), :]
        col_ids = core_ref[0] * half + at + lax.broadcasted_iota(jnp.int32, (TILE, block), 0)
        row_ids = lax.broadcasted_iota(jnp.int32, (TILE, block), 1)
        add_columns(
            part,
            values_at(packed, half + at),
            norms_of(part),
            rows_t[...],
            row_norms[...],
            sums,
            col_ids != row_ids,
        )


def apply_self(core, features, packed):
    block, feat = features.shape
    outs = [
        jax.ShapeDtypeStruct((feat + 8, block), jnp.float32),
        jax.ShapeDtypeStruct((feat, block), jnp.bfloat16),
        jax.ShapeDtypeStruct((1, block), jnp.float32),
    ]
    whole = lambda i, core: (0, 0)
    return pl.pallas_call(
        self_kernel,
        grid_spec=pltpu.PrefetchScalarGridSpec(
            num_scalar_prefetch=1,
            grid=(1,),
            in_specs=[pl.BlockSpec(memory_space=pltpu.HBM), pl.BlockSpec(packed.shape, whole)],
            out_specs=[pl.BlockSpec(x.shape, whole) for x in outs],
            scratch_shapes=[pltpu.VMEM((block, feat), jnp.bfloat16), pltpu.SemaphoreType.DMA],
        ),
        out_shape=outs,
        compiler_params=PARAMS,
        cost_estimate=pl.CostEstimate(
            flops=2 * 2 * block * block // 2 * feat,
            bytes_accessed=4 * 2**20,
            transcendentals=block * block // 2,
        ),
        name="own_block",
    )(core, features, packed)


def partner_kernel(core_ref, here, there, rows_t, row_norms, own_sums, *refs):
    near = refs[: 2 * REACH]
    sums, held, sems = refs[2 * REACH :]
    half = held.shape[1] // 2
    picks = (here, there)
    for turn in range(2):
        distance = picks[turn][0, 0]
        same_way = (distance < 0) == (core_ref[0] == 0)
        chosen = jnp.abs(distance) - 1 + jnp.where(same_way, 0, REACH)
        for slot in range(2 * REACH):

            @pl.when(chosen == slot)
            def _():
                pltpu.make_async_copy(near[slot], held.at[turn], sems.at[turn]).start()

    sums[...] = own_sums[...]
    for turn in range(2):
        pltpu.make_async_copy(near[0], held.at[turn], sems.at[turn]).wait()

        @pl.loop(0, half // TILE, unroll=True)
        def _(step):
            at = pl.multiple_of(step * TILE, TILE)
            part = held[turn, pl.ds(at, TILE), :]
            ids = core_ref[0] * half + at + lax.broadcasted_iota(jnp.int32, (TILE, 1), 0)
            norms = jnp.where(ids < picks[turn][0, 1], norms_of(part), FAR)
            vals = values_at(held.at[turn], half + at)
            add_columns(part, vals, norms, rows_t[...], row_norms[...], sums)


def apply_partners(which, core, here, there, rows_t, row_norms, own_sums, near):
    feat, block = rows_t.shape
    half = block // 2
    if which == "far":
        picked = lambda i, core, here, there: (0, 1 - core[0])
    else:
        picked = lambda i, core, here, there: (0, core[0])
    out = jax.ShapeDtypeStruct((feat + 8, half), jnp.float32)
    return pl.pallas_call(
        partner_kernel,
        grid_spec=pltpu.PrefetchScalarGridSpec(
            num_scalar_prefetch=3,
            grid=(1,),
            in_specs=[
                pl.BlockSpec((feat, half), picked),
                pl.BlockSpec((1, half), picked),
                pl.BlockSpec((feat + 8, half), picked),
            ]
            + [pl.BlockSpec(memory_space=pl.ANY)] * len(near),
            out_specs=pl.BlockSpec(out.shape, lambda i, core, here, there: (0, 0)),
            scratch_shapes=[
                pltpu.VMEM((2, *near[0].shape), jnp.bfloat16),
                pltpu.SemaphoreType.DMA((2,)),
            ],
        ),
        out_shape=out,
        compiler_params=PARAMS,
        cost_estimate=pl.CostEstimate(
            flops=2 * 2 * half * block * feat,
            bytes_accessed=3 * 2**20,
            transcendentals=half * block,
        ),
        name="partners_" + which,
    )(core, here, there, rows_t, row_norms, own_sums, *near)


def field_kernel(scale, sums, far_sums, field, gram):
    sub = field.shape[0]
    degree = jnp.sum(sums[sub:, :] + far_sums[sub:, :], axis=0, keepdims=True)
    field[...] = (sums[:sub, :] + far_sums[:sub, :]) / degree
    terms = lax.dot_general(
        field[...],
        field[...],
        NT,
        precision=lax.Precision.HIGHEST,
        preferred_element_type=jnp.float32,
    )
    gram[...] = (terms * scale).reshape(gram.shape)


def make_field(particles, sums, far_sums):
    sub, half = sums.shape[0] - 8, sums.shape[1]
    outs = [
        jax.ShapeDtypeStruct((sub, half), jnp.float32),
        jax.ShapeDtypeStruct((sub // 8, 8, sub), jnp.float32),
    ]
    return pl.pallas_call(
        functools.partial(field_kernel, 1.0 / particles),
        out_shape=outs,
        compiler_params=PARAMS,
        cost_estimate=pl.CostEstimate(
            flops=12 * sub * sub * half, bytes_accessed=2 * 2**20, transcendentals=0
        ),
        name="field",
    )(sums, far_sums)


def join_kernel(core_ref, own, other, tiles, out, gram):
    @pl.when(pl.program_id(0) == core_ref[0])
    def _():
        out[...] = own[...]

    @pl.when(pl.program_id(0) != core_ref[0])
    def _():
        out[...] = other[...]

    @pl.when(pl.program_id(0) == 0)
    def _():
        gram[...] = tiles[...].reshape(gram.shape)


def join(core, own, other, tiles):
    sub, half = own.shape
    outs = [
        jax.ShapeDtypeStruct((sub, 2 * half), jnp.float32),
        jax.ShapeDtypeStruct((sub, sub), jnp.float32),
    ]
    return pl.pallas_call(
        join_kernel,
        grid_spec=pltpu.PrefetchScalarGridSpec(
            num_scalar_prefetch=1,
            grid=(2,),
            in_specs=[pl.BlockSpec((sub, half), lambda i, core: (0, 0))] * 2
            + [pl.BlockSpec(tiles.shape, lambda i, core: (0, 0, 0))],
            out_specs=[
                pl.BlockSpec((sub, half), lambda i, core: (0, i)),
                pl.BlockSpec((sub, sub), lambda i, core: (0, 0)),
            ],
        ),
        out_shape=outs,
        compiler_params=PARAMS,
        cost_estimate=pl.CostEstimate(flops=0, bytes_accessed=2 * 2**20, transcendentals=0),
        name="join",
    )(core, own, other, tiles)


def exchange(tiles, groups):
    return lax.all_to_all(tiles, "blk", 0, 0, axis_index_groups=groups, tiled=True)


def sum_over_all(tiles):
    count = tiles.shape[0]
    blocks = lax.axis_size("blk")
    near_z = [list(range(i, i + count)) for i in range(0, blocks, count)]
    planes = [list(range(i, blocks, count)) for i in range(count)]
    part = jnp.sum(exchange(tiles, planes), axis=0)
    part = part + swap(part)
    part = jnp.sum(exchange(jnp.broadcast_to(part, tiles.shape), near_z), axis=0)
    return exchange(jnp.broadcast_to(part, tiles.shape), planes)


def swap(x):
    return lax.ppermute(x, "pair", [(0, 1), (1, 0)])


def relay(x):
    blocks = lax.axis_size("blk")
    pairs = []
    for i in range(blocks):
        if i + 1 < blocks:
            pairs.append((2 * i, 2 * i + 2))
            pairs.append((2 * i + 3, 2 * i + 1))
    return lax.ppermute(x, ("blk", "pair"), pairs)


def per_device(features, subspace, offsets, counts):
    block = features.shape[0]
    core = lax.axis_index("pair").astype(jnp.int32).reshape(1)
    here = jnp.concatenate([offsets, counts], axis=1)
    there = swap(here)
    give, keep = pack(core, features, subspace)
    own_sums, rows_t, row_norms = apply_self(core, features, keep)
    kept, swapped = [], []
    for step in range(REACH):
        give, keep = relay(give), relay(keep)
        if step == 0:
            give, there, own_sums, rows_t, row_norms = lax.optimization_barrier(
                (give, there, own_sums, rows_t, row_norms)
            )
        kept.append(keep)
        swapped.append(swap(give))
    near = kept + swapped
    far = apply_partners("far", core, here, there, rows_t, row_norms, own_sums, near)
    far_sums = swap(far)
    sums = apply_partners("near", core, here, there, rows_t, row_norms, own_sums, near)
    field, gram = make_field(float(lax.axis_size("blk") * block), sums, far_sums)
    other = swap(field)
    return tuple(join(core, field, other, sum_over_all(gram)))


def solution(mesh):
    placed = (P("blk", None), P(None, "blk"), P("pair", "blk"), P("pair", "blk"))
    return jax.shard_map(
        per_device, mesh=mesh, in_specs=placed, out_specs=(P(None, "blk"), P()), check_vma=False
    )
```

```python
import functools

import jax
import jax.numpy as jnp
from jax import lax
from jax.experimental import pallas as pl
from jax.experimental.pallas import tpu as pltpu
from jax.sharding import PartitionSpec as P

REACH = 3
TILE = 256
FAR = 1e30
NT = (((1,), (1,)), ((), ()))
PARAMS = pltpu.CompilerParams(vmem_limit_bytes=32 * 2**20)


def pack_kernel(core_ref, feats_ref, field_ref, give, keep):
    half, feat = feats_ref.shape[0] // 2, feats_ref.shape[1]
    for core in range(2):

        @pl.when(core_ref[0] == core)
        def _():
            for packed, start in ((give, (1 - core) * half), (keep, core * half)):
                packed[:half, :] = feats_ref[start : start + half, :]
                for at in range(0, half, feat):
                    packed[half + at : half + at + feat, :] = field_ref[
                        :, start + at : start + at + feat
                    ].astype(jnp.bfloat16)


def pack(core, features, subspace):
    out = jax.ShapeDtypeStruct(features.shape, jnp.bfloat16)
    whole = lambda i, core: (0, 0)
    return pl.pallas_call(
        pack_kernel,
        grid_spec=pltpu.PrefetchScalarGridSpec(
            num_scalar_prefetch=1,
            grid=(1,),
            in_specs=[pl.BlockSpec(x.shape, whole) for x in (features, subspace)],
            out_specs=[pl.BlockSpec(out.shape, whole)] * 2,
        ),
        out_shape=[out, out],
        compiler_params=pltpu.CompilerParams(vmem_limit_bytes=62 * 2**20),
        cost_estimate=pl.CostEstimate(flops=0, bytes_accessed=2 * 2**20, transcendentals=0),
        name="pack",
    )(core, features, subspace)


def norms_of(part):
    wide = part.astype(jnp.float32)
    return jnp.sum(wide * wide, axis=1, keepdims=True) * (1.0 / 256.0)


def add_columns(feats, vals, col_norms, rows_t, row_norms, sums, apart=None):
    sub = vals.shape[0]
    inner = jnp.dot(feats, rows_t, preferred_element_type=jnp.float32)
    weight = jnp.exp(inner - col_norms - row_norms)
    if apart is not None:
        weight = jnp.where(apart, weight, 0.0)
    sums[sub:, :] += jnp.sum(weight.reshape(TILE // 8, 8, weight.shape[1]), axis=0)
    sums[:sub, :] += jnp.dot(vals, weight.astype(jnp.bfloat16), preferred_element_type=jnp.float32)


def values_at(held, start):
    first = held[pl.ds(pl.multiple_of(start, 128), 128), :]
    second = held[pl.ds(pl.multiple_of(start + 128, 128), 128), :]
    return jnp.concatenate([first, second], axis=1)


def self_kernel(core_ref, feats_ref, packed, sums, rows_t, row_norms, feats, sem):
    block = feats_ref.shape[0]
    half = block // 2
    copy = pltpu.make_async_copy(feats_ref, feats, sem)
    copy.start()
    sums[...] = jnp.zeros_like(sums)
    copy.wait()
    for at in range(0, block, TILE):
        wide = feats[at : at + TILE, :].astype(jnp.float32).T
        row_norms[:, at : at + TILE] = jnp.sum(wide * wide, axis=0, keepdims=True) * (1.0 / 256.0)
        rows_t[:, at : at + TILE] = (wide * (1.0 / 128.0)).astype(jnp.bfloat16)

    @pl.loop(0, half // TILE)
    def _(step):
        at = pl.multiple_of(step * TILE, TILE)
        part = packed[pl.ds(at, TILE), :]
        col_ids = core_ref[0] * half + at + lax.broadcasted_iota(jnp.int32, (TILE, block), 0)
        row_ids = lax.broadcasted_iota(jnp.int32, (TILE, block), 1)
        add_columns(
            part,
            values_at(packed, half + at),
            norms_of(part),
            rows_t[...],
            row_norms[...],
            sums,
            col_ids != row_ids,
        )


def apply_self(core, features, packed):
    block, feat = features.shape
    outs = [
        jax.ShapeDtypeStruct((feat + 8, block), jnp.float32),
        jax.ShapeDtypeStruct((feat, block), jnp.bfloat16),
        jax.ShapeDtypeStruct((1, block), jnp.float32),
    ]
    whole = lambda i, core: (0, 0)
    return pl.pallas_call(
        self_kernel,
        grid_spec=pltpu.PrefetchScalarGridSpec(
            num_scalar_prefetch=1,
            grid=(1,),
            in_specs=[pl.BlockSpec(memory_space=pltpu.HBM), pl.BlockSpec(packed.shape, whole)],
            out_specs=[pl.BlockSpec(x.shape, whole) for x in outs],
            scratch_shapes=[pltpu.VMEM((block, feat), jnp.bfloat16), pltpu.SemaphoreType.DMA],
        ),
        out_shape=outs,
        compiler_params=PARAMS,
        cost_estimate=pl.CostEstimate(
            flops=2 * 2 * block * block // 2 * feat,
            bytes_accessed=4 * 2**20,
            transcendentals=block * block // 2,
        ),
        name="own_block",
    )(core, features, packed)


def partner_kernel(core_ref, here, there, rows_t, row_norms, own_sums, *refs):
    near = refs[: 2 * REACH]
    sums, held, sems = refs[2 * REACH :]
    half = held.shape[1] // 2
    picks = (here, there)
    for turn in range(2):
        distance = picks[turn][0, 0]
        same_way = (distance < 0) == (core_ref[0] == 0)
        chosen = jnp.abs(distance) - 1 + jnp.where(same_way, 0, REACH)
        for slot in range(2 * REACH):

            @pl.when(chosen == slot)
            def _():
                pltpu.make_async_copy(near[slot], held.at[turn], sems.at[turn]).start()

    sums[...] = own_sums[...]
    for turn in range(2):
        pltpu.make_async_copy(near[0], held.at[turn], sems.at[turn]).wait()

        @pl.loop(0, half // TILE, unroll=True)
        def _(step):
            at = pl.multiple_of(step * TILE, TILE)
            part = held[turn, pl.ds(at, TILE), :]
            ids = core_ref[0] * half + at + lax.broadcasted_iota(jnp.int32, (TILE, 1), 0)
            norms = jnp.where(ids < picks[turn][0, 1], norms_of(part), FAR)
            vals = values_at(held.at[turn], half + at)
            add_columns(part, vals, norms, rows_t[...], row_norms[...], sums)


def apply_partners(which, core, here, there, rows_t, row_norms, own_sums, near):
    feat, block = rows_t.shape
    half = block // 2
    if which == "far":
        picked = lambda i, core, here, there: (0, 1 - core[0])
    else:
        picked = lambda i, core, here, there: (0, core[0])
    out = jax.ShapeDtypeStruct((feat + 8, half), jnp.float32)
    return pl.pallas_call(
        partner_kernel,
        grid_spec=pltpu.PrefetchScalarGridSpec(
            num_scalar_prefetch=3,
            grid=(1,),
            in_specs=[
                pl.BlockSpec((feat, half), picked),
                pl.BlockSpec((1, half), picked),
                pl.BlockSpec((feat + 8, half), picked),
            ]
            + [pl.BlockSpec(memory_space=pl.ANY)] * len(near),
            out_specs=pl.BlockSpec(out.shape, lambda i, core, here, there: (0, 0)),
            scratch_shapes=[
                pltpu.VMEM((2, *near[0].shape), jnp.bfloat16),
                pltpu.SemaphoreType.DMA((2,)),
            ],
        ),
        out_shape=out,
        compiler_params=PARAMS,
        cost_estimate=pl.CostEstimate(
            flops=2 * 2 * half * block * feat,
            bytes_accessed=3 * 2**20,
            transcendentals=half * block,
        ),
        name="partners_" + which,
    )(core, here, there, rows_t, row_norms, own_sums, *near)


def field_kernel(scale, sums, far_sums, field, gram):
    sub = field.shape[0]
    degree = jnp.sum(sums[sub:, :] + far_sums[sub:, :], axis=0, keepdims=True)
    field[...] = (sums[:sub, :] + far_sums[:sub, :]) / degree
    terms = lax.dot_general(
        field[...],
        field[...],
        NT,
        precision=lax.Precision.HIGHEST,
        preferred_element_type=jnp.float32,
    )
    gram[...] = (terms * scale).reshape(gram.shape)


def make_field(particles, sums, far_sums):
    sub, half = sums.shape[0] - 8, sums.shape[1]
    outs = [
        jax.ShapeDtypeStruct((sub, half), jnp.float32),
        jax.ShapeDtypeStruct((sub // 8, 8, sub), jnp.float32),
    ]
    return pl.pallas_call(
        functools.partial(field_kernel, 1.0 / particles),
        out_shape=outs,
        compiler_params=PARAMS,
        cost_estimate=pl.CostEstimate(
            flops=12 * sub * sub * half, bytes_accessed=2 * 2**20, transcendentals=0
        ),
        name="field",
    )(sums, far_sums)


def join_kernel(core_ref, own, other, tiles, out, gram):
    @pl.when(pl.program_id(0) == core_ref[0])
    def _():
        out[...] = own[...]

    @pl.when(pl.program_id(0) != core_ref[0])
    def _():
        out[...] = other[...]

    @pl.when(pl.program_id(0) == 0)
    def _():
        gram[...] = tiles[...].reshape(gram.shape)


def join(core, own, other, tiles):
    sub, half = own.shape
    outs = [
        jax.ShapeDtypeStruct((sub, 2 * half), jnp.float32),
        jax.ShapeDtypeStruct((sub, sub), jnp.float32),
    ]
    return pl.pallas_call(
        join_kernel,
        grid_spec=pltpu.PrefetchScalarGridSpec(
            num_scalar_prefetch=1,
            grid=(2,),
            in_specs=[pl.BlockSpec((sub, half), lambda i, core: (0, 0))] * 2
            + [pl.BlockSpec(tiles.shape, lambda i, core: (0, 0, 0))],
            out_specs=[
                pl.BlockSpec((sub, half), lambda i, core: (0, i)),
                pl.BlockSpec((sub, sub), lambda i, core: (0, 0)),
            ],
        ),
        out_shape=outs,
        compiler_params=PARAMS,
        cost_estimate=pl.CostEstimate(flops=0, bytes_accessed=2 * 2**20, transcendentals=0),
        name="join",
    )(core, own, other, tiles)


def exchange(tiles, groups):
    return lax.all_to_all(tiles, "blk", 0, 0, axis_index_groups=groups, tiled=True)


def sum_over_all(tiles):
    count = tiles.shape[0]
    blocks = lax.axis_size("blk")
    near_z = [list(range(i, i + count)) for i in range(0, blocks, count)]
    planes = [list(range(i, blocks, count)) for i in range(count)]
    part = jnp.sum(exchange(tiles, planes), axis=0)
    part = part + swap(part)
    part = jnp.sum(exchange(jnp.broadcast_to(part, tiles.shape), near_z), axis=0)
    return exchange(jnp.broadcast_to(part, tiles.shape), planes)


def swap(x):
    return lax.ppermute(x, "pair", [(0, 1), (1, 0)])


def relay(x):
    blocks = lax.axis_size("blk")
    pairs = []
    for i in range(blocks):
        if i + 1 < blocks:
            pairs.append((2 * i, 2 * i + 2))
            pairs.append((2 * i + 3, 2 * i + 1))
    return lax.ppermute(x, ("blk", "pair"), pairs)


def per_device(features, subspace, offsets, counts):
    block = features.shape[0]
    core = lax.axis_index("pair").astype(jnp.int32).reshape(1)
    here = jnp.concatenate([offsets, counts], axis=1)
    give, keep = pack(core, features, subspace)
    own_sums, rows_t, row_norms = apply_self(core, features, keep)
    kept, swapped = [], []
    for step in range(REACH):
        give, keep = relay(give), relay(keep)
        if step == 0:
            give, own_sums, rows_t, row_norms = lax.optimization_barrier(
                (give, own_sums, rows_t, row_norms)
            )
        if step == 1:
            give, swapped[0], here = lax.optimization_barrier((give, swapped[0], here))
        kept.append(keep)
        swapped.append(swap(give))
    there = swap(here)
    near = kept + swapped
    far = apply_partners("far", core, here, there, rows_t, row_norms, own_sums, near)
    far_sums = swap(far)
    sums = apply_partners("near", core, here, there, rows_t, row_norms, own_sums, near)
    field, gram = make_field(float(lax.axis_size("blk") * block), sums, far_sums)
    other = swap(field)
    return tuple(join(core, field, other, sum_over_all(gram)))


def solution(mesh):
    placed = (P("blk", None), P(None, "blk"), P("pair", "blk"), P("pair", "blk"))
    return jax.shard_map(
        per_device, mesh=mesh, in_specs=placed, out_specs=(P(None, "blk"), P()), check_vma=False
    )
```

```python
import functools

import jax
import jax.numpy as jnp
from jax import lax
from jax.experimental import pallas as pl
from jax.experimental.pallas import tpu as pltpu
from jax.sharding import PartitionSpec as P

REACH = 3
TILE = 256
FAR = 1e30
NT = (((1,), (1,)), ((), ()))
PARAMS = pltpu.CompilerParams(vmem_limit_bytes=32 * 2**20)


def pack_kernel(core_ref, feats_ref, field_ref, give, keep):
    half, feat = feats_ref.shape[0] // 2, feats_ref.shape[1]
    for core in range(2):

        @pl.when(core_ref[0] == core)
        def _():
            for packed, start in ((give, (1 - core) * half), (keep, core * half)):
                packed[:half, :] = feats_ref[start : start + half, :]
                for at in range(0, half, feat):
                    packed[half + at : half + at + feat, :] = field_ref[
                        :, start + at : start + at + feat
                    ].astype(jnp.bfloat16)


def pack(core, features, subspace):
    out = jax.ShapeDtypeStruct(features.shape, jnp.bfloat16)
    whole = lambda i, core: (0, 0)
    return pl.pallas_call(
        pack_kernel,
        grid_spec=pltpu.PrefetchScalarGridSpec(
            num_scalar_prefetch=1,
            grid=(1,),
            in_specs=[pl.BlockSpec(x.shape, whole) for x in (features, subspace)],
            out_specs=[pl.BlockSpec(out.shape, whole)] * 2,
        ),
        out_shape=[out, out],
        compiler_params=pltpu.CompilerParams(vmem_limit_bytes=62 * 2**20),
        cost_estimate=pl.CostEstimate(flops=0, bytes_accessed=2 * 2**20, transcendentals=0),
        name="pack",
    )(core, features, subspace)


def norms_of(part):
    wide = part.astype(jnp.float32)
    return jnp.sum(wide * wide, axis=1, keepdims=True) * (1.0 / 256.0)


def add_columns(feats, vals, col_norms, rows_t, row_norms, sums, apart=None):
    sub = vals.shape[0]
    inner = jnp.dot(feats, rows_t, preferred_element_type=jnp.float32)
    weight = jnp.exp(inner - col_norms - row_norms)
    if apart is not None:
        weight = jnp.where(apart, weight, 0.0)
    sums[sub:, :] += jnp.sum(weight.reshape(TILE // 8, 8, weight.shape[1]), axis=0)
    sums[:sub, :] += jnp.dot(vals, weight.astype(jnp.bfloat16), preferred_element_type=jnp.float32)


def values_at(held, start):
    first = held[pl.ds(pl.multiple_of(start, 128), 128), :]
    second = held[pl.ds(pl.multiple_of(start + 128, 128), 128), :]
    return jnp.concatenate([first, second], axis=1)


def self_kernel(core_ref, feats_ref, packed, sums, rows, wide_norms, feats, rows_t, row_norms, sem):
    block = feats_ref.shape[0]
    half = block // 2
    copy = pltpu.make_async_copy(feats_ref, feats, sem)
    copy.start()
    sums[...] = jnp.zeros_like(sums)
    copy.wait()
    for at in range(0, block, TILE):
        wide = feats[at : at + TILE, :].astype(jnp.float32).T
        rows[at : at + TILE, :] = feats[at : at + TILE, :] * (1.0 / 128.0)
        wide_norms[at : at + TILE, :] = jnp.broadcast_to(
            norms_of(feats[at : at + TILE, :]), (TILE, wide_norms.shape[1])
        )
        row_norms[:, at : at + TILE] = jnp.sum(wide * wide, axis=0, keepdims=True) * (1.0 / 256.0)
        rows_t[:, at : at + TILE] = (wide * (1.0 / 128.0)).astype(jnp.bfloat16)

    @pl.loop(0, half // TILE)
    def _(step):
        at = pl.multiple_of(step * TILE, TILE)
        part = packed[pl.ds(at, TILE), :]
        col_ids = core_ref[0] * half + at + lax.broadcasted_iota(jnp.int32, (TILE, block), 0)
        row_ids = lax.broadcasted_iota(jnp.int32, (TILE, block), 1)
        add_columns(
            part,
            values_at(packed, half + at),
            norms_of(part),
            rows_t[...],
            row_norms[...],
            sums,
            col_ids != row_ids,
        )


def apply_self(core, features, packed):
    block, feat = features.shape
    outs = [
        jax.ShapeDtypeStruct((feat + 8, block), jnp.float32),
        jax.ShapeDtypeStruct((block, feat), jnp.bfloat16),
        jax.ShapeDtypeStruct((block, feat), jnp.float32),
    ]
    whole = lambda i, core: (0, 0)
    return pl.pallas_call(
        self_kernel,
        grid_spec=pltpu.PrefetchScalarGridSpec(
            num_scalar_prefetch=1,
            grid=(1,),
            in_specs=[pl.BlockSpec(memory_space=pltpu.HBM), pl.BlockSpec(packed.shape, whole)],
            out_specs=[pl.BlockSpec(x.shape, whole) for x in outs],
            scratch_shapes=[
                pltpu.VMEM((block, feat), jnp.bfloat16),
                pltpu.VMEM((feat, block), jnp.bfloat16),
                pltpu.VMEM((1, block), jnp.float32),
                pltpu.SemaphoreType.DMA,
            ],
        ),
        out_shape=outs,
        compiler_params=PARAMS,
        cost_estimate=pl.CostEstimate(
            flops=2 * 2 * block * block // 2 * feat,
            bytes_accessed=4 * 2**20,
            transcendentals=block * block // 2,
        ),
        name="own_block",
    )(core, features, packed)


def partner_kernel(core_ref, here, there, rows, wide_norms, own_sums, *refs):
    near = refs[: 2 * REACH]
    sums, acc, deg, held, sems = refs[2 * REACH :]
    feat = rows.shape[1]
    half = held.shape[1] // 2
    picks = (here, there)
    for turn in range(2):
        distance = picks[turn][0, 0]
        same_way = (distance < 0) == (core_ref[0] == 0)
        chosen = jnp.abs(distance) - 1 + jnp.where(same_way, 0, REACH)
        for slot in range(2 * REACH):

            @pl.when(chosen == slot)
            def _():
                pltpu.make_async_copy(near[slot], held.at[turn], sems.at[turn]).start()

    acc[...] = jnp.zeros_like(acc)
    deg[...] = jnp.zeros_like(deg)
    for turn in range(2):
        pltpu.make_async_copy(near[0], held.at[turn], sems.at[turn]).wait()

        @pl.loop(0, half // TILE, unroll=True)
        def _(step):
            at = pl.multiple_of(step * TILE, TILE)
            part = held[turn, pl.ds(at, TILE), :]
            wide = part.astype(jnp.float32)
            norms = jnp.sum((wide * wide).T, axis=0, keepdims=True) * (1.0 / 256.0)
            ids = core_ref[0] * half + at + lax.broadcasted_iota(jnp.int32, (1, TILE), 1)
            norms = jnp.where(ids < picks[turn][0, 1], norms, FAR)
            inner = lax.dot_general(rows[...], part, NT, preferred_element_type=jnp.float32)
            both = jnp.concatenate([wide_norms[...], wide_norms[...]], axis=1)
            weight = jnp.exp(inner - norms - both)
            deg[...] += weight[:, :feat] + weight[:, feat:]
            acc[...] += lax.dot_general(
                weight.astype(jnp.bfloat16),
                values_at(held.at[turn], half + at),
                NT,
                preferred_element_type=jnp.float32,
            )

    sums[:feat, :] = own_sums[:feat, :] + acc[...].T
    sums[feat:, :] = own_sums[feat:, :] + jnp.sum(
        deg[...].T.reshape(feat // 8, 8, deg.shape[0]), axis=0
    )


def apply_partners(which, core, here, there, rows, wide_norms, own_sums, near):
    block, feat = rows.shape
    half = block // 2
    if which == "far":
        choose = lambda core: 1 - core[0]
    else:
        choose = lambda core: core[0]
    out = jax.ShapeDtypeStruct((feat + 8, half), jnp.float32)
    return pl.pallas_call(
        partner_kernel,
        grid_spec=pltpu.PrefetchScalarGridSpec(
            num_scalar_prefetch=3,
            grid=(1,),
            in_specs=[
                pl.BlockSpec((half, feat), lambda i, core, here, there: (choose(core), 0)),
                pl.BlockSpec((half, feat), lambda i, core, here, there: (choose(core), 0)),
                pl.BlockSpec((feat + 8, half), lambda i, core, here, there: (0, choose(core))),
            ]
            + [pl.BlockSpec(memory_space=pl.ANY)] * len(near),
            out_specs=pl.BlockSpec(out.shape, lambda i, core, here, there: (0, 0)),
            scratch_shapes=[
                pltpu.VMEM((half, feat), jnp.float32),
                pltpu.VMEM((half, feat), jnp.float32),
                pltpu.VMEM((2, *near[0].shape), jnp.bfloat16),
                pltpu.SemaphoreType.DMA((2,)),
            ],
        ),
        out_shape=out,
        compiler_params=PARAMS,
        cost_estimate=pl.CostEstimate(
            flops=2 * 2 * half * block * feat,
            bytes_accessed=3 * 2**20,
            transcendentals=half * block,
        ),
        name="partners_" + which,
    )(core, here, there, rows, wide_norms, own_sums, *near)


def field_kernel(scale, sums, far_sums, field, gram):
    sub = field.shape[0]
    degree = jnp.sum(sums[sub:, :] + far_sums[sub:, :], axis=0, keepdims=True)
    field[...] = (sums[:sub, :] + far_sums[:sub, :]) / degree
    terms = lax.dot_general(
        field[...],
        field[...],
        NT,
        precision=lax.Precision.HIGHEST,
        preferred_element_type=jnp.float32,
    )
    gram[...] = (terms * scale).reshape(gram.shape)


def make_field(particles, sums, far_sums):
    sub, half = sums.shape[0] - 8, sums.shape[1]
    outs = [
        jax.ShapeDtypeStruct((sub, half), jnp.float32),
        jax.ShapeDtypeStruct((sub // 8, 8, sub), jnp.float32),
    ]
    return pl.pallas_call(
        functools.partial(field_kernel, 1.0 / particles),
        out_shape=outs,
        compiler_params=PARAMS,
        cost_estimate=pl.CostEstimate(
            flops=12 * sub * sub * half, bytes_accessed=2 * 2**20, transcendentals=0
        ),
        name="field",
    )(sums, far_sums)


def join_kernel(core_ref, own, other, tiles, out, gram):
    @pl.when(pl.program_id(0) == core_ref[0])
    def _():
        out[...] = own[...]

    @pl.when(pl.program_id(0) != core_ref[0])
    def _():
        out[...] = other[...]

    @pl.when(pl.program_id(0) == 0)
    def _():
        gram[...] = tiles[...].reshape(gram.shape)


def join(core, own, other, tiles):
    sub, half = own.shape
    outs = [
        jax.ShapeDtypeStruct((sub, 2 * half), jnp.float32),
        jax.ShapeDtypeStruct((sub, sub), jnp.float32),
    ]
    return pl.pallas_call(
        join_kernel,
        grid_spec=pltpu.PrefetchScalarGridSpec(
            num_scalar_prefetch=1,
            grid=(2,),
            in_specs=[pl.BlockSpec((sub, half), lambda i, core: (0, 0))] * 2
            + [pl.BlockSpec(tiles.shape, lambda i, core: (0, 0, 0))],
            out_specs=[
                pl.BlockSpec((sub, half), lambda i, core: (0, i)),
                pl.BlockSpec((sub, sub), lambda i, core: (0, 0)),
            ],
        ),
        out_shape=outs,
        compiler_params=PARAMS,
        cost_estimate=pl.CostEstimate(flops=0, bytes_accessed=2 * 2**20, transcendentals=0),
        name="join",
    )(core, own, other, tiles)


def exchange(tiles, groups):
    return lax.all_to_all(tiles, "blk", 0, 0, axis_index_groups=groups, tiled=True)


def sum_over_all(tiles):
    count = tiles.shape[0]
    blocks = lax.axis_size("blk")
    near_z = [list(range(i, i + count)) for i in range(0, blocks, count)]
    planes = [list(range(i, blocks, count)) for i in range(count)]
    part = jnp.sum(exchange(tiles, planes), axis=0)
    part = part + swap(part)
    part = jnp.sum(exchange(jnp.broadcast_to(part, tiles.shape), near_z), axis=0)
    return exchange(jnp.broadcast_to(part, tiles.shape), planes)


def swap(x):
    return lax.ppermute(x, "pair", [(0, 1), (1, 0)])


def relay(x):
    blocks = lax.axis_size("blk")
    pairs = []
    for i in range(blocks):
        if i + 1 < blocks:
            pairs.append((2 * i, 2 * i + 2))
            pairs.append((2 * i + 3, 2 * i + 1))
    return lax.ppermute(x, ("blk", "pair"), pairs)


def per_device(features, subspace, offsets, counts):
    block = features.shape[0]
    core = lax.axis_index("pair").astype(jnp.int32).reshape(1)
    here = jnp.concatenate([offsets, counts], axis=1)
    give, keep = pack(core, features, subspace)
    own_sums, rows, wide_norms = apply_self(core, features, keep)
    kept, swapped = [], []
    for step in range(REACH):
        give, keep = relay(give), relay(keep)
        if step == 0:
            give, own_sums, rows, wide_norms = lax.optimization_barrier(
                (give, own_sums, rows, wide_norms)
            )
        if step == 1:
            give, swapped[0], here = lax.optimization_barrier((give, swapped[0], here))
        kept.append(keep)
        swapped.append(swap(give))
    there = swap(here)
    near = kept + swapped
    far = apply_partners("far", core, here, there, rows, wide_norms, own_sums, near)
    far_sums = swap(far)
    sums = apply_partners("near", core, here, there, rows, wide_norms, own_sums, near)
    field, gram = make_field(float(lax.axis_size("blk") * block), sums, far_sums)
    other = swap(field)
    return tuple(join(core, field, other, sum_over_all(gram)))


def solution(mesh):
    placed = (P("blk", None), P(None, "blk"), P("pair", "blk"), P("pair", "blk"))
    return jax.shard_map(
        per_device, mesh=mesh, in_specs=placed, out_specs=(P(None, "blk"), P()), check_vma=False
    )
```

```python
import functools

import jax
import jax.numpy as jnp
from jax import lax
from jax.experimental import pallas as pl
from jax.experimental.pallas import tpu as pltpu
from jax.sharding import PartitionSpec as P

REACH = 3
TILE = 256
FAR = 1e30
NT = (((1,), (1,)), ((), ()))
PARAMS = pltpu.CompilerParams(vmem_limit_bytes=32 * 2**20)


def pack_kernel(core_ref, feats_ref, field_ref, give, keep):
    half, feat = feats_ref.shape[0] // 2, feats_ref.shape[1]
    for core in range(2):

        @pl.when(core_ref[0] == core)
        def _():
            for packed, start in ((give, (1 - core) * half), (keep, core * half)):
                packed[:half, :] = feats_ref[start : start + half, :]
                for at in range(0, half, feat):
                    packed[half + at : half + at + feat, :] = field_ref[
                        :, start + at : start + at + feat
                    ].astype(jnp.bfloat16)


def pack(core, features, subspace):
    out = jax.ShapeDtypeStruct(features.shape, jnp.bfloat16)
    whole = lambda i, core: (0, 0)
    return pl.pallas_call(
        pack_kernel,
        grid_spec=pltpu.PrefetchScalarGridSpec(
            num_scalar_prefetch=1,
            grid=(1,),
            in_specs=[pl.BlockSpec(x.shape, whole) for x in (features, subspace)],
            out_specs=[pl.BlockSpec(out.shape, whole)] * 2,
        ),
        out_shape=[out, out],
        compiler_params=pltpu.CompilerParams(vmem_limit_bytes=62 * 2**20),
        cost_estimate=pl.CostEstimate(flops=0, bytes_accessed=2 * 2**20, transcendentals=0),
        name="pack",
    )(core, features, subspace)


def norms_of(part):
    wide = part.astype(jnp.float32)
    return jnp.sum(wide * wide, axis=1, keepdims=True) * (1.0 / 256.0)


def add_columns(feats, vals, col_norms, rows_t, row_norms, sums, apart=None):
    sub = vals.shape[0]
    inner = jnp.dot(feats, rows_t, preferred_element_type=jnp.float32)
    weight = jnp.exp(inner - col_norms - row_norms)
    if apart is not None:
        weight = jnp.where(apart, weight, 0.0)
    sums[sub:, :] += jnp.sum(weight.reshape(TILE // 8, 8, weight.shape[1]), axis=0)
    sums[:sub, :] += jnp.dot(vals, weight.astype(jnp.bfloat16), preferred_element_type=jnp.float32)


def values_at(held, start):
    first = held[pl.ds(pl.multiple_of(start, 128), 128), :]
    second = held[pl.ds(pl.multiple_of(start + 128, 128), 128), :]
    return jnp.concatenate([first, second], axis=1)


def self_kernel(core_ref, feats_ref, packed, sums, rows, wide_norms, feats, rows_t, row_norms, sem):
    block = feats_ref.shape[0]
    half = block // 2
    copy = pltpu.make_async_copy(feats_ref, feats, sem)
    copy.start()
    sums[...] = jnp.zeros_like(sums)
    copy.wait()
    for at in range(0, block, TILE):
        wide = feats[at : at + TILE, :].astype(jnp.float32).T
        rows[at : at + TILE, :] = feats[at : at + TILE, :] * (1.0 / 128.0)
        wide_norms[at : at + TILE, :] = jnp.broadcast_to(
            norms_of(feats[at : at + TILE, :]), (TILE, wide_norms.shape[1])
        )
        row_norms[:, at : at + TILE] = jnp.sum(wide * wide, axis=0, keepdims=True) * (1.0 / 256.0)
        rows_t[:, at : at + TILE] = (wide * (1.0 / 128.0)).astype(jnp.bfloat16)

    @pl.loop(0, half // TILE)
    def _(step):
        at = pl.multiple_of(step * TILE, TILE)
        part = packed[pl.ds(at, TILE), :]
        col_ids = core_ref[0] * half + at + lax.broadcasted_iota(jnp.int32, (TILE, block), 0)
        row_ids = lax.broadcasted_iota(jnp.int32, (TILE, block), 1)
        add_columns(
            part,
            values_at(packed, half + at),
            norms_of(part),
            rows_t[...],
            row_norms[...],
            sums,
            col_ids != row_ids,
        )


def apply_self(core, features, packed):
    block, feat = features.shape
    outs = [
        jax.ShapeDtypeStruct((feat + 8, block), jnp.float32),
        jax.ShapeDtypeStruct((block, feat), jnp.bfloat16),
        jax.ShapeDtypeStruct((block, feat), jnp.float32),
    ]
    whole = lambda i, core: (0, 0)
    return pl.pallas_call(
        self_kernel,
        grid_spec=pltpu.PrefetchScalarGridSpec(
            num_scalar_prefetch=1,
            grid=(1,),
            in_specs=[pl.BlockSpec(memory_space=pltpu.HBM), pl.BlockSpec(packed.shape, whole)],
            out_specs=[pl.BlockSpec(x.shape, whole) for x in outs],
            scratch_shapes=[
                pltpu.VMEM((block, feat), jnp.bfloat16),
                pltpu.VMEM((feat, block), jnp.bfloat16),
                pltpu.VMEM((1, block), jnp.float32),
                pltpu.SemaphoreType.DMA,
            ],
        ),
        out_shape=outs,
        compiler_params=PARAMS,
        cost_estimate=pl.CostEstimate(
            flops=2 * 2 * block * block // 2 * feat,
            bytes_accessed=4 * 2**20,
            transcendentals=block * block // 2,
        ),
        name="own_block",
    )(core, features, packed)


def partner_kernel(core_ref, here, there, rows, wide_norms, own_sums, *refs):
    near = refs[: 2 * REACH]
    sums, acc, deg, held, sems = refs[2 * REACH :]
    feat = rows.shape[1]
    half = held.shape[1] // 2
    picks = (here, there)
    for turn in range(2):
        distance = picks[turn][0, 0]
        same_way = (distance < 0) == (core_ref[0] == 0)
        chosen = jnp.abs(distance) - 1 + jnp.where(same_way, 0, REACH)
        for slot in range(2 * REACH):

            @pl.when(chosen == slot)
            def _():
                pltpu.make_async_copy(near[slot], held.at[turn], sems.at[turn]).start()

    acc[...] = jnp.zeros_like(acc)
    deg[...] = jnp.zeros_like(deg)
    for turn in range(2):
        pltpu.make_async_copy(near[0], held.at[turn], sems.at[turn]).wait()

        @pl.loop(0, half // TILE, unroll=True)
        def _(step):
            at = pl.multiple_of(step * TILE, TILE)
            part = held[turn, pl.ds(at, TILE), :]
            wide = part.astype(jnp.float32)
            norms = jnp.sum((wide * wide).T, axis=0, keepdims=True) * (1.0 / 256.0)
            ids = core_ref[0] * half + at + lax.broadcasted_iota(jnp.int32, (1, TILE), 1)
            norms = jnp.where(ids < picks[turn][0, 1], norms, FAR)
            inner = lax.dot_general(rows[...], part, NT, preferred_element_type=jnp.float32)
            both = jnp.concatenate([wide_norms[...], wide_norms[...]], axis=1)
            weight = jnp.exp(inner - norms - both)
            deg[...] += weight[:, :feat] + weight[:, feat:]
            acc[...] += lax.dot_general(
                weight.astype(jnp.bfloat16),
                values_at(held.at[turn], half + at),
                NT,
                preferred_element_type=jnp.float32,
            )

    sums[:feat, :] = own_sums[:feat, :] + acc[...].T
    sums[feat:, :] = own_sums[feat:, :] + jnp.sum(
        deg[...].T.reshape(feat // 8, 8, deg.shape[0]), axis=0
    )


def apply_partners(which, core, here, there, rows, wide_norms, own_sums, near):
    block, feat = rows.shape
    half = block // 2
    if which == "far":
        choose = lambda core: 1 - core[0]
    else:
        choose = lambda core: core[0]
    out = jax.ShapeDtypeStruct((feat + 8, half), jnp.float32)
    return pl.pallas_call(
        partner_kernel,
        grid_spec=pltpu.PrefetchScalarGridSpec(
            num_scalar_prefetch=3,
            grid=(1,),
            in_specs=[
                pl.BlockSpec((half, feat), lambda i, core, here, there: (choose(core), 0)),
                pl.BlockSpec((half, feat), lambda i, core, here, there: (choose(core), 0)),
                pl.BlockSpec((feat + 8, half), lambda i, core, here, there: (0, choose(core))),
            ]
            + [pl.BlockSpec(memory_space=pl.ANY)] * len(near),
            out_specs=pl.BlockSpec(out.shape, lambda i, core, here, there: (0, 0)),
            scratch_shapes=[
                pltpu.VMEM((half, feat), jnp.float32),
                pltpu.VMEM((half, feat), jnp.float32),
                pltpu.VMEM((2, *near[0].shape), jnp.bfloat16),
                pltpu.SemaphoreType.DMA((2,)),
            ],
        ),
        out_shape=out,
        compiler_params=PARAMS,
        cost_estimate=pl.CostEstimate(
            flops=2 * 2 * half * block * feat,
            bytes_accessed=3 * 2**20,
            transcendentals=half * block,
        ),
        name="partners_" + which,
    )(core, here, there, rows, wide_norms, own_sums, *near)


def field_kernel(scale, sums, far_sums, field, gram):
    sub = field.shape[0]
    degree = jnp.sum(sums[sub:, :] + far_sums[sub:, :], axis=0, keepdims=True)
    field[...] = (sums[:sub, :] + far_sums[:sub, :]) / degree
    terms = lax.dot_general(
        field[...],
        field[...],
        NT,
        precision=lax.Precision.HIGHEST,
        preferred_element_type=jnp.float32,
    )
    gram[...] = (terms * scale).reshape(gram.shape)


def make_field(particles, sums, far_sums):
    sub, half = sums.shape[0] - 8, sums.shape[1]
    outs = [
        jax.ShapeDtypeStruct((sub, half), jnp.float32),
        jax.ShapeDtypeStruct((sub // 8, 8, sub), jnp.float32),
    ]
    return pl.pallas_call(
        functools.partial(field_kernel, 1.0 / particles),
        out_shape=outs,
        compiler_params=PARAMS,
        cost_estimate=pl.CostEstimate(
            flops=12 * sub * sub * half, bytes_accessed=2 * 2**20, transcendentals=0
        ),
        name="field",
    )(sums, far_sums)


def join_kernel(core_ref, own, other, tiles, out, gram):
    @pl.when(pl.program_id(0) == core_ref[0])
    def _():
        out[...] = own[...]

    @pl.when(pl.program_id(0) != core_ref[0])
    def _():
        out[...] = other[...]

    @pl.when(pl.program_id(0) == 0)
    def _():
        gram[...] = tiles[...].reshape(gram.shape)


def join(core, own, other, tiles):
    sub, half = own.shape
    outs = [
        jax.ShapeDtypeStruct((sub, 2 * half), jnp.float32),
        jax.ShapeDtypeStruct((sub, sub), jnp.float32),
    ]
    return pl.pallas_call(
        join_kernel,
        grid_spec=pltpu.PrefetchScalarGridSpec(
            num_scalar_prefetch=1,
            grid=(2,),
            in_specs=[pl.BlockSpec((sub, half), lambda i, core: (0, 0))] * 2
            + [pl.BlockSpec(tiles.shape, lambda i, core: (0, 0, 0))],
            out_specs=[
                pl.BlockSpec((sub, half), lambda i, core: (0, i)),
                pl.BlockSpec((sub, sub), lambda i, core: (0, 0)),
            ],
        ),
        out_shape=outs,
        compiler_params=PARAMS,
        cost_estimate=pl.CostEstimate(flops=0, bytes_accessed=2 * 2**20, transcendentals=0),
        name="join",
    )(core, own, other, tiles)


def exchange(tiles, groups):
    return lax.all_to_all(tiles, "blk", 0, 0, axis_index_groups=groups, tiled=True)


def sum_over_all(tiles):
    count = tiles.shape[0]
    blocks = lax.axis_size("blk")
    near_z = [list(range(i, i + count)) for i in range(0, blocks, count)]
    planes = [list(range(i, blocks, count)) for i in range(count)]
    part = jnp.sum(exchange(tiles, planes), axis=0)
    part = part + swap(part)
    part = jnp.sum(exchange(jnp.broadcast_to(part, tiles.shape), near_z), axis=0)
    return exchange(jnp.broadcast_to(part, tiles.shape), planes)


def swap(x):
    return lax.ppermute(x, "pair", [(0, 1), (1, 0)])


def relay(x):
    blocks = lax.axis_size("blk")
    pairs = []
    for i in range(blocks):
        if i + 1 < blocks:
            pairs.append((2 * i, 2 * i + 2))
            pairs.append((2 * i + 3, 2 * i + 1))
    return lax.ppermute(x, ("blk", "pair"), pairs)


def per_device(features, subspace, offsets, counts):
    block = features.shape[0]
    core = lax.axis_index("pair").astype(jnp.int32).reshape(1)
    here = jnp.concatenate([offsets, counts], axis=1)
    give, keep = pack(core, features, subspace)
    own_sums, rows, wide_norms = apply_self(core, features, keep)
    kept, given = [], []
    for step in range(REACH):
        give, keep = relay(give), relay(keep)
        if step == 0:
            give, own_sums, rows, wide_norms = lax.optimization_barrier(
                (give, own_sums, rows, wide_norms)
            )
        kept.append(keep)
        given.append(give)
        if step == 1:
            keep, given[0], given[1], here = lax.optimization_barrier((keep, *given, here))
            kept[1] = keep
    swapped = [swap(x) for x in given]
    there = swap(here)
    near = kept + swapped
    far = apply_partners("far", core, here, there, rows, wide_norms, own_sums, near)
    far_sums = swap(far)
    sums = apply_partners("near", core, here, there, rows, wide_norms, own_sums, near)
    field, gram = make_field(float(lax.axis_size("blk") * block), sums, far_sums)
    other = swap(field)
    return tuple(join(core, field, other, sum_over_all(gram)))


def solution(mesh):
    placed = (P("blk", None), P(None, "blk"), P("pair", "blk"), P("pair", "blk"))
    return jax.shard_map(
        per_device, mesh=mesh, in_specs=placed, out_specs=(P(None, "blk"), P()), check_vma=False
    )
```
